128 devices in a mesh: seq: 16 (over x, y), dp: 4 (over z), rep: 2 (over core).
Axes of the slice: x: 4, y: 4, z: 4, core: 2. Of those that a mesh axis runs over, the one named last changes fastest.
Arguments:
- hidden: bfloat16 [4, 8192, 8192], P('dp', 'seq'), may hold values from -6 to 6
- kept: int32 [4, 16, 192], P('dp'), may hold values from 0 to 511, as said below
- counts: int32 [4, 16], P('dp'), may hold values from 48 to 192, as said below
- queries: bfloat16 [4, 3072, 4096], P('dp', 'seq', 'rep'), may hold values from -6 to 6
- keys: bfloat16 [4, 3072, 512], P('dp', 'seq', 'rep'), may hold values from -6 to 6
- values: bfloat16 [4, 3072, 512], P('dp', 'seq', 'rep'), may hold values from -6 to 6
- out_grad: bfloat16 [4, 3072, 4096], P('dp', 'seq', 'rep'), may hold values from -6 to 6
- kv_weight: bfloat16 [8192, 2, 512], P('dp', None, 'rep'), may hold values from -0.0625 to 0.0625
Outputs:
- grad_queries: bfloat16 [4, 3072, 4096], P('dp', 'seq', 'rep')
- grad_hidden: bfloat16 [4, 8192, 8192], P('dp', 'seq', 'rep')
- grad_kv_weight: float32 [8192, 2, 512], P(('seq', 'dp'), None, 'rep')
The draws below stay inside these ranges and needn't reach their ends.
Inputs may be any that keep to these rules, and one draw needn't show every extreme that they name: `counts`: in every sequence some shard keeps exactly 192 tokens. `kept`: the first counts[b, s] entries of a shard's list are distinct token indices of that shard in rising order; the other entries are arbitrary token indices.
All inputs are finite; a program needn't handle non-finite values.
Results may differ from the reference program's by a relative error of at most 0.012.
Values may be sent and summed in bfloat16 or wider, within the bound.
No kernel may reach another device: no remote copies, remote signals or barrier semaphores. Data moves between devices by JAX's collectives and lax.ppermute only.
A program may use at most 128 MiB of HBM per device.

```python
import jax
import jax.numpy as jnp
from jax import lax

D = 8192
HEADS = 32
KV_HEADS = 4
HEAD = 128
TOK_DEV = 512
KEEP_CAP = 192
SEQS = 4
SEQ_LEN = 8192
ROWS = 3072
N_SEQ = 16


def shuffled_head(subkey):
    return jax.random.permutation(subkey, TOK_DEV)[:KEEP_CAP]


def draw_lists(key):
    draws = jax.random.randint(jax.random.fold_in(key, 11), (SEQS, N_SEQ), KEEP_CAP // 4, KEEP_CAP + 1)
    chosen = jax.random.randint(jax.random.fold_in(key, 12), (SEQS,), 0, N_SEQ)
    full_shard = jnp.arange(N_SEQ)[None, :] == chosen[:, None]
    shard_counts = jnp.where(full_shard, KEEP_CAP, draws).astype(jnp.int32)
    subkeys = jax.random.split(jax.random.fold_in(key, 13), SEQS * N_SEQ)
    picks = jax.vmap(shuffled_head)(subkeys).reshape(SEQS, N_SEQ, KEEP_CAP)
    slot_index = jnp.arange(KEEP_CAP)[None, None, :]
    ranked = jnp.sort(jnp.where(slot_index < shard_counts[:, :, None], picks, picks + TOK_DEV), axis=2)
    lists = jnp.where(ranked >= TOK_DEV, ranked - TOK_DEV, ranked).astype(jnp.int32)
    return (lists, shard_counts)


def key_rows(key):
    shape = (SEQS, ROWS, KV_HEADS * HEAD)
    normal_part = jnp.clip(jax.random.normal(jax.random.fold_in(key, 21), shape, jnp.float32), -6.0, 6.0)
    base = normal_part
    return base


def draw_kept(key, part):
    lists, shard_counts = draw_lists(key)
    return lists


def draw_counts(key, part):
    lists, shard_counts = draw_lists(key)
    return shard_counts


def draw_keys(key, part):
    return key_rows(key).astype(jnp.bfloat16)


def draw_queries(key, part):
    key = jax.random.fold_in(key, 31)
    shape = (SEQS, ROWS, HEADS * HEAD)
    normal_part = jnp.clip(jax.random.normal(jax.random.fold_in(key, 1), shape, jnp.float32), -6.0, 6.0)
    base = normal_part
    return base.astype(jnp.bfloat16)


def level_of(key, shape, pieces, low, top_value):
    gain, own = 1.0, jax.random.fold_in(key, 6)
    for axis_at, parts in pieces:
        steps = jnp.exp(jax.random.uniform(jax.random.fold_in(own, axis_at), (parts,), jnp.float32, low / len(pieces), top_value / len(pieces)))
        gain = gain * jnp.repeat(steps, shape[axis_at] // parts).reshape([-1 if axis == axis_at else 1 for axis in range(len(shape))])
    return gain


def bell_draw(rng, shape, scale, bound, cuts=(), kind=jnp.bfloat16):
    result = scale * jax.random.normal(rng, shape, jnp.float32)
    if cuts:
        result = result * level_of(rng, shape, cuts, -0.22, 0.18)
    return jnp.clip(result, -bound, bound).astype(kind)


def setup_inputs(seed: int = 0) -> dict:
    splits = jax.random.split(jax.random.key(seed), 9)
    hidden = bell_draw(splits[0], (SEQS, SEQ_LEN, D), 1.0, 6.0, ((0, 4), (1, 16)))
    kept = draw_kept(jax.random.fold_in(splits[8], 71), 0)
    counts = draw_counts(jax.random.fold_in(splits[8], 71), 0)
    queries = draw_queries(jax.random.fold_in(splits[8], 71), 0)
    keys = draw_keys(jax.random.fold_in(splits[8], 71), 0)
    values = bell_draw(splits[5], (SEQS, ROWS, KV_HEADS * HEAD), 1.0, 6.0, ((0, 4), (1, 16), (2, 2)))
    out_grad = bell_draw(splits[6], (SEQS, ROWS, HEADS * HEAD), 1.0, 6.0, ((0, 4), (1, 16), (2, 2)))
    kv_weight = bell_draw(splits[7], (D, 2, KV_HEADS * HEAD), D ** -0.5, 0.0625, ((0, 4), (2, 2)))
    return dict(hidden=hidden, kept=kept, counts=counts, queries=queries, keys=keys, values=values, out_grad=out_grad, kv_weight=kv_weight)


def head_backward(query_head, key_head, value_head, dout_head, allowed, factor):
    scores = jnp.dot(query_head, key_head.T, preferred_element_type=jnp.float32) * factor
    masked = jnp.where(allowed, scores, jnp.float32(-1e30))
    highest = jnp.max(masked, axis=1, keepdims=True)
    exponent = jnp.where(allowed, jnp.exp(masked - highest), jnp.float32(0.0))
    sum_exp = jnp.sum(exponent, axis=1, keepdims=True)
    probs = exponent / jnp.where(sum_exp > 0, sum_exp, jnp.float32(1.0))
    prob_grad = jnp.dot(dout_head, value_head.T, preferred_element_type=jnp.float32)
    row_delta = jnp.sum(probs * prob_grad, axis=1, keepdims=True)
    dscore = (probs * (prob_grad - row_delta)).astype(jnp.bfloat16)
    probs_low = probs.astype(jnp.bfloat16)
    query_grad = (jnp.dot(dscore, key_head, preferred_element_type=jnp.float32) * factor).astype(jnp.bfloat16)
    key_part = (jnp.dot(dscore.T, query_head, preferred_element_type=jnp.float32) * factor).astype(jnp.bfloat16)
    value_part = jnp.dot(probs_low.T, dout_head, preferred_element_type=jnp.float32).astype(jnp.bfloat16)
    return query_grad, key_part, value_part


def reference(hidden, kept, counts, queries, keys, values, out_grad, kv_weight):
    factor = HEAD ** -0.5
    group_size = HEADS // KV_HEADS
    slot_index = jnp.arange(KEEP_CAP, dtype=jnp.int32)
    shard_index = jnp.arange(N_SEQ, dtype=jnp.int32)
    weight_total = jnp.zeros((D, 2, KV_HEADS * HEAD), jnp.float32)
    query_list = []
    input_list = []
    for sequence in range(SEQS):
        is_live = (slot_index[None, :] < counts[sequence][:, None]).reshape(ROWS)
        position = (shard_index[:, None] * TOK_DEV + kept[sequence]).reshape(ROWS).astype(jnp.int32)
        allowed = is_live[:, None] & is_live[None, :] & (position[None, :] <= position[:, None])
        query_heads = queries[sequence].reshape(ROWS, HEADS, HEAD).transpose(1, 0, 2)
        dout_heads = out_grad[sequence].reshape(ROWS, HEADS, HEAD).transpose(1, 0, 2)
        key_heads = keys[sequence].reshape(ROWS, KV_HEADS, HEAD).transpose(1, 0, 2)
        value_heads = values[sequence].reshape(ROWS, KV_HEADS, HEAD).transpose(1, 0, 2)

        def one_head(head_index):
            shared = head_index // group_size
            return head_backward(query_heads[head_index], key_heads[shared], value_heads[shared], dout_heads[head_index], allowed, factor)

        query_grad, key_part, value_part = lax.map(one_head, jnp.arange(HEADS, dtype=jnp.int32))
        query_list.append(query_grad.transpose(1, 0, 2).reshape(ROWS, HEADS * HEAD))
        key_sum = jnp.sum(key_part.astype(jnp.float32).reshape(KV_HEADS, group_size, ROWS, HEAD), axis=1)
        value_sum = jnp.sum(value_part.astype(jnp.float32).reshape(KV_HEADS, group_size, ROWS, HEAD), axis=1)
        kv_grad = jnp.stack([key_sum.transpose(1, 0, 2).reshape(ROWS, KV_HEADS * HEAD), value_sum.transpose(1, 0, 2).reshape(ROWS, KV_HEADS * HEAD)], axis=1).astype(jnp.bfloat16)
        gathered = jnp.take(hidden[sequence], position, axis=0)
        weight_total = weight_total + jnp.einsum("rd,rck->dck", gathered.astype(jnp.float32), kv_grad.astype(jnp.float32))
        input_rows = jnp.einsum("rck,dck->rd", kv_grad.astype(jnp.float32), kv_weight.astype(jnp.float32)).astype(jnp.bfloat16)
        target = jnp.where(is_live, position, SEQ_LEN).astype(jnp.int32)
        input_list.append(jnp.zeros((SEQ_LEN, D), jnp.bfloat16).at[target].set(input_rows, mode="drop"))
    return jnp.stack(query_list, axis=0), jnp.stack(input_list, axis=0), weight_total
```

```python
import functools

import jax
import jax.numpy as jnp
from jax import lax
from jax.experimental import pallas as pl
from jax.experimental.pallas import tpu as pltpu
from jax.sharding import PartitionSpec as P

HEAD = 128
MASKED = -1e30
LOG2E = 1.4426950408889634
ROWS_ROWS = (((1,), (1,)), ((), ()))
ROWS_COLS = (((1,), (0,)), ((), ()))
TILE = 512
VMEM_BYTES = 48 * 1024 * 1024


def pack_kernel(q_ref, do_ref, k_ref, v_ref, out_ref):
    out_ref[0, :, 0:HEAD] = q_ref[...]
    out_ref[0, :, HEAD : 2 * HEAD] = do_ref[...]
    out_ref[0, :, 2 * HEAD : 3 * HEAD] = k_ref[...]
    out_ref[0, :, 3 * HEAD : 4 * HEAD] = v_ref[...]


def pack_heads(queries, out_grad, keys, values):
    capacity, width = queries.shape
    heads = width // HEAD
    group = heads // (keys.shape[1] // HEAD)
    own = pl.BlockSpec((capacity, HEAD), lambda h: (0, h))
    shared = pl.BlockSpec((capacity, HEAD), lambda h: (0, h // group))
    return pl.pallas_call(
        pack_kernel,
        grid=(heads,),
        out_shape=jax.ShapeDtypeStruct((heads, capacity, 4 * HEAD), queries.dtype),
        in_specs=[own, own, shared, shared],
        out_specs=pl.BlockSpec((1, capacity, 4 * HEAD), lambda h: (h, 0, 0)),
        cost_estimate=pl.CostEstimate(flops=0, bytes_accessed=6_000_000, transcendentals=0),
        name="pack_heads",
    )(queries, out_grad, keys, values)


def gather_kernel(rows_ref, hidden_ref, out_ref):
    capacity, tokens = out_ref.shape[1], hidden_ref.shape[0]
    token = lax.broadcasted_iota(jnp.int32, (capacity, tokens), 1)
    pick = (token == rows_ref[...]).astype(jnp.bfloat16)
    picked = lax.dot_general(
        pick, hidden_ref[...], ROWS_COLS, preferred_element_type=jnp.float32
    ).astype(jnp.bfloat16)
    for part in range(out_ref.shape[0]):
        out_ref[part] = picked[:, part * HEAD : (part + 1) * HEAD]


def gather_columns(rows, hidden, parts):
    capacity = rows.shape[0]
    tokens, width = hidden.shape
    steps = width // (parts * HEAD)
    return pl.pallas_call(
        gather_kernel,
        grid=(steps,),
        out_shape=jax.ShapeDtypeStruct((parts, capacity, width // parts), hidden.dtype),
        in_specs=[
            pl.BlockSpec((capacity, 1), lambda s: (0, 0)),
            pl.BlockSpec((tokens, parts * HEAD), lambda s: (0, s)),
        ],
        out_specs=pl.BlockSpec((parts, capacity, HEAD), lambda s: (0, 0, s)),
        cost_estimate=pl.CostEstimate(
            flops=1_600_000_000, bytes_accessed=12_000_000, transcendentals=0
        ),
        name="gather_columns",
    )(rows[:, None], hidden)


def attention_kernel(
    counts, x, dq_out, dkv_out, q_s, k_s, kt_s, v_s, do_s, s_s, g_s, dq_s, dk_s, dv_s, *, shards, cap
):
    bf, f32 = jnp.bfloat16, jnp.float32
    scale = HEAD**-0.5
    row = lax.broadcasted_iota(jnp.int32, (cap, HEAD), 0)
    lane = lax.broadcasted_iota(jnp.int32, (cap, HEAD), 1)
    zero = jnp.zeros((cap, HEAD), bf)
    offsets = []
    total = jnp.int32(0)
    for s in range(shards):
        offsets.append(total)
        total = total + ((counts[s] + 15) // 16) * 16
    end = pl.ds(pl.multiple_of(total, 16), TILE)
    empty = jnp.zeros((TILE, HEAD), bf)
    q_s[end, :HEAD] = empty
    q_s[end, HEAD:] = empty
    do_s[end, :] = empty
    v_s[end, :] = empty
    k_s[end, :HEAD] = empty
    end_lane = lax.broadcasted_iota(jnp.int32, (TILE, HEAD), 1)
    k_s[end, HEAD:] = jnp.where(end_lane == 0, MASKED, 0.0).astype(bf)
    one = jnp.where(lane == 0, 1.0, 0.0).astype(bf)
    for s in range(shards):
        at = pl.ds(pl.multiple_of(offsets[s], 16), cap)
        here = slice(s * cap, (s + 1) * cap)
        live = row < counts[s]
        q_s[at, :HEAD] = jnp.where(live, x[here, 0:HEAD], zero)
        q_s[at, HEAD:] = one
        do_s[at, :] = jnp.where(live, x[here, HEAD : 2 * HEAD], zero)
        k_s[at, :HEAD] = jnp.where(live, x[here, 2 * HEAD : 3 * HEAD], zero)
        k_s[at, HEAD:] = jnp.where(live, 0.0, jnp.where(lane == 0, MASKED, 0.0)).astype(bf)
        v_s[at, :] = jnp.where(live, x[here, 3 * HEAD : 4 * HEAD], zero)
    tiles = (total + TILE - 1) // TILE

    def tile_at(index):
        return pl.ds(pl.multiple_of(index * TILE, TILE), TILE)

    def prepare(j, carry):
        at = tile_at(j)
        kt_s[:, at] = k_s[at, :HEAD].T
        dk_s[at, :] = jnp.zeros((TILE, HEAD), f32)
        dv_s[at, :] = jnp.zeros((TILE, HEAD), f32)
        return carry

    lax.fori_loop(0, tiles, prepare, 0)
    key_row = lax.broadcasted_iota(jnp.int32, (TILE, TILE), 0)
    query_lane = lax.broadcasted_iota(jnp.int32, (TILE, TILE), 1)

    def query_step(i, carry):
        q = q_s[tile_at(i), :]
        do = do_s[tile_at(i), :]

        def scan(j, state, diagonal):
            high, total_e, total_w = state
            at = tile_at(j)
            scores = lax.dot_general(k_s[at, :], q, ROWS_ROWS, preferred_element_type=f32)
            grads = lax.dot_general(v_s[at, :], do, ROWS_ROWS, preferred_element_type=f32)
            scores = scores * (scale * LOG2E)
            if diagonal:
                scores = jnp.where(query_lane >= key_row, scores, MASKED)
            s_s[at, :] = scores
            g_s[at, :] = grads
            new = jnp.maximum(high, jnp.max(scores, axis=0, keepdims=True))
            e = jnp.exp2(scores - new)
            shrink = jnp.exp2(high - new)
            return (
                new,
                total_e * shrink + jnp.sum(e, axis=0, keepdims=True),
                total_w * shrink + jnp.sum(e * grads, axis=0, keepdims=True),
            )

        state = (
            jnp.full((1, TILE), MASKED, f32),
            jnp.zeros((1, TILE), f32),
            jnp.zeros((1, TILE), f32),
        )
        state = lax.fori_loop(0, i, functools.partial(scan, diagonal=False), state)
        high, total_e, total_w = scan(i, state, True)
        delta = total_w / total_e
        log_total = high + jnp.log2(total_e)

        def spread(j, dq):
            at = tile_at(j)
            probs = jnp.exp2(s_s[at, :] - log_total)
            dscore = (probs * (g_s[at, :] - delta)).astype(bf)
            dv_s[at, :] += lax.dot_general(
                probs.astype(bf), do, ROWS_COLS, preferred_element_type=f32
            )
            dk_s[at, :] += lax.dot_general(
                dscore, q[:, :HEAD], ROWS_COLS, preferred_element_type=f32
            )
            return dq + lax.dot_general(
                kt_s[:, at], dscore, ROWS_COLS, preferred_element_type=f32
            )

        dq = lax.fori_loop(0, i + 1, spread, jnp.zeros((HEAD, TILE), f32))
        dq_s[tile_at(i), :] = (dq * scale).T.astype(bf)
        return carry

    lax.fori_loop(0, tiles, query_step, 0)
    for s in range(shards):
        at = pl.ds(pl.multiple_of(offsets[s], 16), cap)
        here = slice(s * cap, (s + 1) * cap)
        live = row < counts[s]
        dq_out[here, :] = jnp.where(live, dq_s[at, :], zero)
        dkv_out[here, :HEAD] = jnp.where(live, dk_s[at, :] * scale, 0.0).astype(bf)
        dkv_out[here, HEAD:] = jnp.where(live, dv_s[at, :], 0.0).astype(bf)


def attention_backward(counts, rows):
    shards, total = counts.shape[0], rows.shape[0]
    padded = -(-(total + TILE) // TILE) * TILE
    bf, f32 = jnp.bfloat16, jnp.float32
    vmem = pl.BlockSpec(memory_space=pltpu.VMEM)
    return pl.pallas_call(
        functools.partial(attention_kernel, shards=shards, cap=total // shards),
        out_shape=(
            jax.ShapeDtypeStruct((total, HEAD), bf),
            jax.ShapeDtypeStruct((total, 2 * HEAD), bf),
        ),
        in_specs=[pl.BlockSpec(memory_space=pltpu.SMEM), vmem],
        out_specs=(vmem, vmem),
        scratch_shapes=[
            pltpu.VMEM((padded, 2 * HEAD), bf),
            pltpu.VMEM((padded, 2 * HEAD), bf),
            pltpu.VMEM((HEAD, padded), bf),
            pltpu.VMEM((padded, HEAD), bf),
            pltpu.VMEM((padded, HEAD), bf),
            pltpu.VMEM((padded, TILE), f32),
            pltpu.VMEM((padded, TILE), f32),
            pltpu.VMEM((padded, HEAD), bf),
            pltpu.VMEM((padded, HEAD), f32),
            pltpu.VMEM((padded, HEAD), f32),
        ],
        compiler_params=pltpu.CompilerParams(vmem_limit_bytes=VMEM_BYTES),
        cost_estimate=pl.CostEstimate(
            flops=6_000_000_000, bytes_accessed=6_000_000, transcendentals=10_000_000
        ),
        name="attention_backward",
    )(counts, rows)


def spread_kernel(order, target_ref, *refs):
    parts, out_ref = refs[:-1], refs[-1]
    step = pl.program_id(0)
    tokens, capacity = out_ref.shape[0], parts[0].shape[0]
    token = lax.broadcasted_iota(jnp.int32, (tokens, capacity), 0)
    pick = (token == target_ref[...]).astype(jnp.bfloat16)
    for index, part in enumerate(parts):

        @pl.when(step == index)
        def _(part=part):
            out_ref[...] = lax.dot_general(
                pick, part[...], ROWS_COLS, preferred_element_type=jnp.float32
            ).astype(jnp.bfloat16)


def spread_rows(order, target, parts, tokens):
    capacity, width = parts[0].shape
    whole = pl.BlockSpec((capacity, width), lambda s, order: (0, 0))
    return pl.pallas_call(
        spread_kernel,
        grid_spec=pltpu.PrefetchScalarGridSpec(
            num_scalar_prefetch=1,
            grid=(len(parts),),
            in_specs=[pl.BlockSpec((1, capacity), lambda s, order: (0, 0))] + [whole] * len(parts),
            out_specs=pl.BlockSpec((tokens, width), lambda s, order: (0, order[s])),
        ),
        out_shape=jax.ShapeDtypeStruct((tokens, width * len(parts)), jnp.bfloat16),
        cost_estimate=pl.CostEstimate(
            flops=800_000_000, bytes_accessed=6_000_000, transcendentals=0
        ),
        name="spread_rows",
    )(order, target[None, :], *parts)


def shards(hidden, kept, counts, queries, keys, values, out_grad, kv_weight):
    bf, f32 = jnp.bfloat16, jnp.float32
    seq_devices = lax.axis_size("seq")
    dp_devices = lax.axis_size("dp")
    rep_devices = lax.axis_size("rep")
    seq_index = lax.axis_index("seq")
    dp_index = lax.axis_index("dp")
    rep_index = lax.axis_index("rep")
    capacity = queries.shape[1]
    tokens_local = hidden.shape[1]
    local_groups = keys.shape[2] // HEAD
    group_size = seq_devices // local_groups
    width = kv_weight.shape[2]
    part_rows = kv_weight.shape[0] // rep_devices

    packed = pack_heads(queries[0], out_grad[0], keys[0], values[0])
    rows = lax.all_to_all(packed, "seq", split_axis=0, concat_axis=0, tiled=True)

    own_rows = lax.dynamic_index_in_dim(kept[0], seq_index, 0, keepdims=False)
    own_count = lax.dynamic_index_in_dim(counts[0], seq_index, 0, keepdims=False)
    columns = gather_columns(own_rows, hidden[0], dp_devices)

    def shift_dp(array, step):
        return lax.ppermute(array, "dp", [(i, (i + step) % dp_devices) for i in range(dp_devices)])

    gathered = []
    for step in range(dp_devices):
        part = lax.dynamic_index_in_dim(
            columns, (dp_index + step) % dp_devices, 0, keepdims=False
        )
        gathered.append(shift_dp(part, step) if step else part)
    halves = kv_weight.reshape(rep_devices, part_rows, 2 * width)
    swap = [(i, (i + 1) % rep_devices) for i in range(rep_devices)]
    kept_half = lax.dynamic_index_in_dim(halves, rep_index, 0, keepdims=False)
    sent_half = lax.dynamic_index_in_dim(halves, 1 - rep_index, 0, keepdims=False)
    weight = jnp.concatenate([kept_half, lax.ppermute(sent_half, "rep", swap)], axis=1)

    grad_query, grad_kv = attention_backward(
        counts[0], rows.reshape(seq_devices * capacity, 4 * HEAD)
    )
    back_kv = lax.all_to_all(
        grad_kv.reshape(seq_devices, capacity, 2 * HEAD), "seq", split_axis=0, concat_axis=0, tiled=True
    )
    grad_query, back_kv = lax.optimization_barrier((grad_query, back_kv))
    back_query = lax.all_to_all(
        grad_query.reshape(seq_devices, capacity, HEAD), "seq", split_axis=0, concat_axis=0, tiled=True
    )
    back_query = back_query.transpose(1, 0, 2).reshape(capacity, seq_devices * HEAD)

    group_sum = jnp.sum(
        back_kv.reshape(local_groups, group_size, capacity, 2, HEAD).astype(f32), axis=1
    )
    kv_grad = group_sum.transpose(1, 2, 0, 3).reshape(capacity, 2 * width).astype(bf)

    kv_all = [kv_grad] + [shift_dp(kv_grad, step) for step in range(1, dp_devices)]
    kv_all = jnp.concatenate(kv_all, axis=0)

    terms = lax.dot_general(
        jnp.concatenate(gathered, axis=0), kv_all, (((0,), (0,)), ((), ())), preferred_element_type=f32
    ).astype(bf)
    terms = lax.all_to_all(
        terms.reshape(seq_devices, -1, 2 * width), "seq", split_axis=0, concat_axis=0, tiled=True
    )
    grad_weight = jnp.sum(terms.astype(f32), axis=0).reshape(-1, 2, width)

    kv_both = jnp.concatenate([kv_all, lax.ppermute(kv_all, "rep", swap)], axis=1)
    products = lax.dot_general(
        kv_both, weight, (((1,), (1,)), ((), ())), preferred_element_type=f32
    ).astype(bf)
    products = products.reshape(dp_devices, capacity, part_rows)
    dp_per_rep = dp_devices // rep_devices
    lane_of = (dp_index % dp_per_rep) * rep_devices + rep_index
    received = []
    for step in range(dp_devices):
        pairs = []
        for dp in range(dp_devices):
            for rep in range(rep_devices):
                lane = (dp % dp_per_rep) * rep_devices + rep
                to_dp = (lane + step) % dp_devices
                pairs.append((dp * rep_devices + rep, to_dp * rep_devices + dp // dp_per_rep))
        want = (lane_of + step) % dp_devices
        block = lax.dynamic_index_in_dim(
            products, (dp_index - want) % dp_devices, 0, keepdims=False
        )
        received.append(lax.ppermute(block, ("dp", "rep"), pairs))
    order = jnp.stack([(dp_index - step) % dp_devices for step in range(dp_devices)]).astype(jnp.int32)
    slot_index = jnp.arange(capacity, dtype=jnp.int32)
    target = jnp.where(slot_index < own_count, own_rows, tokens_local)
    grad_hidden = spread_rows(order, target, received, tokens_local)
    return (back_query[None], grad_hidden[None], grad_weight)


def solution(mesh):
    placed = (
        P("dp", "seq", None),
        P("dp", None, None),
        P("dp", None),
        P("dp", "seq", "rep"),
        P("dp", "seq", "rep"),
        P("dp", "seq", "rep"),
        P("dp", "seq", "rep"),
        P("dp", None, "rep"),
    )
    return jax.shard_map(
        shards,
        mesh=mesh,
        in_specs=placed,
        out_specs=(P("dp", "seq", "rep"), P("dp", "seq", "rep"), P(("seq", "dp"), None, "rep")),
        check_vma=False,
    )
```

```python
import functools

import jax
import jax.numpy as jnp
from jax import lax
from jax.experimental import pallas as pl
from jax.experimental.pallas import tpu as pltpu
from jax.sharding import PartitionSpec as P

HEAD = 128
MASKED = -1e30
LOG2E = 1.4426950408889634
ROWS_ROWS = (((1,), (1,)), ((), ()))
ROWS_COLS = (((1,), (0,)), ((), ()))
QT = 512
KT = 512
VMEM_BYTES = 56 * 1024 * 1024
SIDE = 4


def gather_kernel(place, rows_ref, hidden_ref, out_ref, pick_ref):
    capacity, tokens = rows_ref.shape[0], hidden_ref.shape[0]

    @pl.when(pl.program_id(0) == 0)
    def _():
        token = lax.broadcasted_iota(jnp.int32, (capacity, tokens), 1)
        pick_ref[...] = (token == rows_ref[...]).astype(jnp.bfloat16)

    picked = lax.dot_general(
        pick_ref[...], hidden_ref[...], ROWS_COLS, preferred_element_type=jnp.float32
    ).astype(jnp.bfloat16)
    parts = out_ref.shape[0]
    for part in range(parts):
        for block in range(out_ref.shape[2] // HEAD):
            first = (block * parts + part) * HEAD
            out_ref[part, :, block * HEAD : (block + 1) * HEAD] = picked[:, first : first + HEAD]


def gather_columns(place, rows, hidden, parts, cores):
    capacity = rows.shape[0]
    tokens, width = hidden.shape
    half = width // cores
    steps = 4
    block = half // steps
    return pl.pallas_call(
        gather_kernel,
        grid_spec=pltpu.PrefetchScalarGridSpec(
            num_scalar_prefetch=1,
            grid=(steps,),
            in_specs=[
                pl.BlockSpec((capacity, 1), lambda s, place: (0, 0)),
                pl.BlockSpec((tokens, block), lambda s, place: (0, place[4] * steps + s)),
            ],
            out_specs=pl.BlockSpec((parts, capacity, block // parts), lambda s, place: (0, 0, s)),
            scratch_shapes=[pltpu.VMEM((capacity, tokens), jnp.bfloat16)],
        ),
        out_shape=jax.ShapeDtypeStruct((parts, capacity, half // parts), hidden.dtype),
        cost_estimate=pl.CostEstimate(
            flops=800_000_000, bytes_accessed=6_000_000, transcendentals=0
        ),
        name="gather_columns",
    )(place, rows[:, None], hidden)


def y_sum_kernel(place, *refs):
    parts, outs = refs[:4], refs[4:]
    cap = outs[0].shape[0]
    for step, out in enumerate(outs):
        at = pl.ds(pl.multiple_of(((place[0] + step) % len(outs)) * cap, 64), cap)
        total = parts[0][at, :].astype(jnp.float32)
        for part in parts[1:]:
            total = total + part[at, :].astype(jnp.float32)
        out[...] = total.astype(jnp.bfloat16)


def y_sum(place, parts):
    rows, width = parts[0].shape
    vmem = pl.BlockSpec(memory_space=pltpu.VMEM)
    return pl.pallas_call(
        y_sum_kernel,
        in_specs=[pl.BlockSpec(memory_space=pltpu.SMEM)] + [vmem] * len(parts),
        out_specs=[vmem] * len(parts),
        out_shape=[jax.ShapeDtypeStruct((rows // len(parts), width), jnp.bfloat16)] * len(parts),
        cost_estimate=pl.CostEstimate(
            flops=1_000_000, bytes_accessed=2_000_000, transcendentals=0
        ),
        name="y_sum",
    )(place, *parts)


def x_sum_kernel(place, *refs):
    parts, out_ref, by_x = refs[:-2], refs[-2], refs[-1]
    cap = out_ref.shape[0]
    count = len(parts)
    groups = out_ref.shape[1] // (2 * HEAD)
    for step, part in enumerate(parts):
        at = pl.ds(pl.multiple_of(((place[0] - step) % count) * cap, 64), cap)
        by_x[at, :] = part[...].astype(jnp.float32)
    size = count // groups
    for group in range(groups):
        total = by_x[group * size * cap : (group * size + 1) * cap, :]
        for x in range(group * size + 1, (group + 1) * size):
            total = total + by_x[x * cap : (x + 1) * cap, :]
        total = total.astype(jnp.bfloat16)
        for kind in range(2):
            first = (kind * groups + group) * HEAD
            out_ref[:, first : first + HEAD] = total[:, kind * HEAD : (kind + 1) * HEAD]


def x_sum(place, parts, groups):
    rows, width = parts[0].shape
    vmem = pl.BlockSpec(memory_space=pltpu.VMEM)
    return pl.pallas_call(
        x_sum_kernel,
        in_specs=[pl.BlockSpec(memory_space=pltpu.SMEM)] + [vmem] * len(parts),
        out_specs=vmem,
        out_shape=jax.ShapeDtypeStruct((rows, groups * width), jnp.bfloat16),
        scratch_shapes=[pltpu.VMEM((rows * len(parts), width), jnp.float32)],
        cost_estimate=pl.CostEstimate(
            flops=1_000_000, bytes_accessed=1_000_000, transcendentals=0
        ),
        name="x_sum",
    )(place, *parts)


def terms_kernel(place, own_ref, other_ref, *refs):
    kv, (out_ref, columns_s, kv_s) = refs[:-3], refs[-3:]
    count, cap = len(kv), kv[0].shape[0]
    step = pl.program_id(0)

    def collect(columns_ref):
        for index in range(count):
            held = (place[3] - index) % count
            columns_s[index * cap : (index + 1) * cap, :] = columns_ref[held]

    @pl.when(step == 0)
    def _():
        collect(own_ref)
        for index, part in enumerate(kv):
            kv_s[index * cap : (index + 1) * cap, :] = part[...]

    @pl.when(step == 1)
    def _():
        collect(other_ref)

    out_ref[...] = lax.dot_general(
        columns_s[...], kv_s[...], (((0,), (0,)), ((), ())), preferred_element_type=jnp.float32
    ).astype(jnp.bfloat16)


def weight_terms(place, own, other, kv):
    count, cap, half = own.shape
    width = kv[0].shape[1]
    columns = pl.BlockSpec((count, cap, half), lambda s, place: (0, 0, 0))
    return pl.pallas_call(
        terms_kernel,
        grid_spec=pltpu.PrefetchScalarGridSpec(
            num_scalar_prefetch=1,
            grid=(2,),
            in_specs=[columns] * 2
            + [pl.BlockSpec((cap, width), lambda s, place: (0, 0))] * len(kv),
            out_specs=pl.BlockSpec((half, width), lambda s, place: ((s + place[4]) % 2, 0)),
            scratch_shapes=[
                pltpu.VMEM((count * cap, half), jnp.bfloat16),
                pltpu.VMEM((count * cap, width), jnp.bfloat16),
            ],
        ),
        out_shape=jax.ShapeDtypeStruct((2 * half, width), jnp.bfloat16),
        compiler_params=pltpu.CompilerParams(vmem_limit_bytes=VMEM_BYTES),
        cost_estimate=pl.CostEstimate(
            flops=1_600_000_000, bytes_accessed=6_000_000, transcendentals=0
        ),
        name="weight_terms",
    )(place, own, other, *kv)


def products_kernel(place, *refs):
    w_own, w_other, out_s, kv_s = refs[-4:]
    count = (len(refs) - 4) // 3
    own, other, parts = refs[:count], refs[count : 2 * count], refs[2 * count : 3 * count]
    cap, half = own[0].shape
    for index in range(count):
        kv_s[index * cap : (index + 1) * cap, :half] = own[index][...]
        kv_s[index * cap : (index + 1) * cap, half:] = other[index][...]
    chunk = 256
    for first in range(0, out_s.shape[1], chunk):
        here = slice(first, first + chunk)
        total = lax.dot_general(
            kv_s[:, :half], w_own[here, :], ROWS_ROWS, preferred_element_type=jnp.float32
        ) + lax.dot_general(
            kv_s[:, half:], w_other[here, :], ROWS_ROWS, preferred_element_type=jnp.float32
        )
        out_s[:, here] = total.astype(jnp.bfloat16)
    for step, part in enumerate(parts):
        held = (place[3] - place[5] - step) % count
        part[...] = out_s[pl.ds(pl.multiple_of(held * cap, 64), cap), :]


def input_products(place, own, other, w_own, w_other):
    cap, half = own[0].shape
    count, width = len(own), w_own.shape[0]
    vmem = pl.BlockSpec(memory_space=pltpu.VMEM)

    def body(place, *refs):
        ins, outs, scratch = refs[: 2 * count + 2], refs[2 * count + 2 : 3 * count + 2], refs[3 * count + 2 :]
        products_kernel(place, *ins[: 2 * count], *outs, ins[-2], ins[-1], *scratch)

    return pl.pallas_call(
        body,
        in_specs=[pl.BlockSpec(memory_space=pltpu.SMEM)] + [vmem] * (2 * count + 2),
        out_specs=[vmem] * count,
        out_shape=[jax.ShapeDtypeStruct((cap, width), jnp.bfloat16)] * count,
        scratch_shapes=[
            pltpu.VMEM((count * cap, width), jnp.bfloat16),
            pltpu.VMEM((count * cap, 2 * half), jnp.bfloat16),
        ],
        compiler_params=pltpu.CompilerParams(vmem_limit_bytes=VMEM_BYTES),
        cost_estimate=pl.CostEstimate(
            flops=1_600_000_000, bytes_accessed=6_000_000, transcendentals=0
        ),
        name="input_products",
    )(place, *own, *other, w_own, w_other)


def attention_kernel(counts, place, q_own, do_own, far, kv0, kv1, kv2, kv3,
                     dq_own, dq_far, out0, out1, out2, out3,
                     kv_s, k_s, kt_s, v_s, q_s, do_s, tri_s, s_s, g_s, so_s, go_s, dq_s, dk_s, dv_s, off_s):
    bf, f32 = jnp.bfloat16, jnp.float32
    cap = q_own.shape[0]
    far_heads = far.shape[1] // (2 * HEAD)
    shards = counts.shape[0]
    side = 4
    scale = HEAD**-0.5
    x_at, y_at, group = place[0], place[1], place[2]
    row = lax.broadcasted_iota(jnp.int32, (cap, HEAD), 0)
    lane = lax.broadcasted_iota(jnp.int32, (cap, HEAD), 1)
    zero = jnp.zeros((cap, HEAD), bf)

    def up16(value):
        return ((value + 15) // 16) * 16

    block = side * cap
    for index, ref in enumerate((kv0, kv1, kv2, kv3)):
        kv_s[index * block : (index + 1) * block, :] = ref[...]
    total = jnp.int32(0)
    for s in range(shards):
        off_s[s] = total
        at = pl.ds(pl.multiple_of(total, 16), cap)
        held = ((y_at - s % side) % side) * side + (x_at - s // side) % side
        pair = kv_s[pl.ds(pl.multiple_of(held * cap, 64), cap), :]
        live = row < counts[s]
        k_s[at, :HEAD] = jnp.where(live, pair[:, :HEAD], zero)
        k_s[at, HEAD:] = jnp.where(live, 0.0, jnp.where(lane == 0, MASKED, 0.0)).astype(bf)
        v_s[at, :] = jnp.where(live, pair[:, HEAD:], zero)
        total = total + up16(counts[s])
    end = pl.ds(pl.multiple_of(total, 16), KT)
    k_s[end, :HEAD] = jnp.zeros((KT, HEAD), bf)
    k_s[end, HEAD:] = jnp.zeros((KT, HEAD), bf)
    v_s[end, :] = jnp.zeros((KT, HEAD), bf)

    def k_at(index):
        return pl.ds(pl.multiple_of(index * KT, KT), KT)

    def prepare(j, carry):
        at = k_at(j)
        kt_s[:, at] = k_s[at, :HEAD].T
        dk_s[at, :] = jnp.zeros((KT, HEAD), f32)
        dv_s[at, :] = jnp.zeros((KT, HEAD), f32)
        return carry

    lax.fori_loop(0, (total + cap + KT - 1) // KT, prepare, 0)
    one_lane = lax.broadcasted_iota(jnp.int32, (QT, HEAD), 1)
    ones = jnp.where(one_lane == 0, 1.0, 0.0).astype(bf)
    slot = lax.broadcasted_iota(jnp.int32, (cap, 2 * HEAD), 0)
    key_slot = lax.broadcasted_iota(jnp.int32, (cap, 2 * HEAD), 1)
    later = jnp.where(key_slot > slot, MASKED, 0.0).astype(bf)
    same = jnp.where(key_slot == slot, 1.0, 0.0).astype(bf)
    key_row = lax.broadcasted_iota(jnp.int32, (KT, QT), 0)

    def one_shard(shard, q_ref, do_ref, q_first, do_first, dq_ref):
        count = counts[shard]
        before = pl.multiple_of(off_s[shard], 16)
        rows = up16(count)
        live = row < count
        for h in range(far_heads):
            at = pl.ds(pl.multiple_of(h * rows, 16), cap)
            q_here = pl.ds(pl.multiple_of(q_first + h * HEAD, HEAD), HEAD)
            do_here = pl.ds(pl.multiple_of(do_first + h * HEAD, HEAD), HEAD)
            q_s[at, :] = jnp.where(live, q_ref[:, q_here], zero)
            do_s[at, :] = jnp.where(live, do_ref[:, do_here], zero)
            tri_s[at, :] = later
        tail = pl.ds(pl.multiple_of(far_heads * rows, 16), QT)
        q_s[tail, :] = jnp.zeros((QT, HEAD), bf)
        do_s[tail, :] = jnp.zeros((QT, HEAD), bf)
        tri_s[tail, :] = jnp.zeros((QT, 2 * HEAD), bf)
        own = pl.ds(before, cap)
        full = before // KT
        rest = before - full * KT
        tiles = (far_heads * rows + QT - 1) // QT

        def query_step(i, carry):
            q_at = pl.ds(pl.multiple_of(i * QT, QT), QT)
            q = q_s[q_at, :]
            do = do_s[q_at, :]
            q_one = jnp.concatenate([q, ones], axis=1)
            own_k = k_s[own, :HEAD]
            scores = lax.dot_general(own_k, q, ROWS_ROWS, preferred_element_type=f32) * (scale * LOG2E)
            scores = scores + lax.dot_general(same, tri_s[q_at, :], ROWS_ROWS, preferred_element_type=f32)
            grads = lax.dot_general(v_s[own, :], do, ROWS_ROWS, preferred_element_type=f32)
            so_s[...] = scores
            go_s[...] = grads
            high = jnp.max(scores, axis=0, keepdims=True)
            e = jnp.exp2(scores - high)
            state = (high, jnp.sum(e, axis=0, keepdims=True), jnp.sum(e * grads, axis=0, keepdims=True))

            def scan(j, state, partial):
                high, total_e, total_w = state
                at = k_at(j)
                scores = lax.dot_general(k_s[at, :], q_one, ROWS_ROWS, preferred_element_type=f32)
                grads = lax.dot_general(v_s[at, :], do, ROWS_ROWS, preferred_element_type=f32)
                scores = scores * (scale * LOG2E)
                if partial:
                    scores = jnp.where(key_row < rest, scores, MASKED)
                s_s[at, :] = scores
                g_s[at, :] = grads
                new = jnp.maximum(high, jnp.max(scores, axis=0, keepdims=True))
                e = jnp.exp2(scores - new)
                shrink = jnp.exp2(high - new)
                return (
                    new,
                    total_e * shrink + jnp.sum(e, axis=0, keepdims=True),
                    total_w * shrink + jnp.sum(e * grads, axis=0, keepdims=True),
                )

            state = lax.fori_loop(0, full, functools.partial(scan, partial=False), state)
            ends = full + (rest > 0).astype(jnp.int32)
            high, total_e, total_w = lax.fori_loop(full, ends, functools.partial(scan, partial=True), state)
            delta = total_w / total_e
            log_total = high + jnp.log2(total_e)

            def spread(at, key_t, scores, grads):
                probs = jnp.exp2(scores - log_total)
                dscore = (probs * (grads - delta)).astype(bf)
                dv_s[at, :] += lax.dot_general(probs.astype(bf), do, ROWS_COLS, preferred_element_type=f32)
                dk_s[at, :] += lax.dot_general(dscore, q, ROWS_COLS, preferred_element_type=f32)
                return lax.dot_general(key_t, dscore, ROWS_COLS, preferred_element_type=f32)

            dq = spread(own, own_k.T, so_s[...], go_s[...])
            dq = lax.fori_loop(
                0, ends, lambda j, dq: dq + spread(k_at(j), kt_s[:, k_at(j)], s_s[k_at(j), :], g_s[k_at(j), :]), dq
            )
            dq_s[q_at, :] = (dq * scale).T.astype(bf)
            return carry

        lax.fori_loop(0, tiles, query_step, 0)
        for h in range(far_heads):
            at = pl.ds(pl.multiple_of(h * rows, 16), cap)
            dq_ref[:, h * HEAD : (h + 1) * HEAD] = jnp.where(live, dq_s[at, :], zero)

    span = far_heads * HEAD
    one_shard(x_at * side + y_at, q_own, do_own, group * span, group * span, dq_own)
    one_shard((side - 1 - x_at) * side + y_at, far, far, 0, span, dq_far)

    for step, ref in enumerate((out0, out1, out2, out3)):
        for x in range(side):
            shard = x * side + (y_at + step) % side
            at = pl.ds(pl.multiple_of(off_s[shard], 16), cap)
            here = slice(x * cap, (x + 1) * cap)
            live = row < counts[shard]
            ref[here, :HEAD] = jnp.where(live, dk_s[at, :] * scale, 0.0).astype(bf)
            ref[here, HEAD:] = jnp.where(live, dv_s[at, :], 0.0).astype(bf)


def attention_backward(counts, place, q_own, do_own, far, kvs):
    cap, width = far.shape[0], far.shape[1] // 2
    shards = counts.shape[0]
    rows = shards * cap
    keys = -(-(rows + KT) // KT) * KT
    queries = -(-(cap * (width // HEAD) + max(QT, cap)) // QT) * QT
    bf, f32 = jnp.bfloat16, jnp.float32
    vmem = pl.BlockSpec(memory_space=pltpu.VMEM)
    smem = pl.BlockSpec(memory_space=pltpu.SMEM)
    block = kvs[0].shape
    return pl.pallas_call(
        attention_kernel,
        out_shape=[jax.ShapeDtypeStruct((cap, width), bf)] * 2 + [jax.ShapeDtypeStruct(block, bf)] * 4,
        in_specs=[smem, smem] + [vmem] * 7,
        out_specs=[vmem] * 6,
        scratch_shapes=[
            pltpu.VMEM((rows, 2 * HEAD), bf),
            pltpu.VMEM((keys, 2 * HEAD), bf),
            pltpu.VMEM((HEAD, keys), bf),
            pltpu.VMEM((keys, HEAD), bf),
            pltpu.VMEM((queries, HEAD), bf),
            pltpu.VMEM((queries, HEAD), bf),
            pltpu.VMEM((queries, 2 * HEAD), bf),
            pltpu.VMEM((keys, QT), f32),
            pltpu.VMEM((keys, QT), f32),
            pltpu.VMEM((cap, QT), f32),
            pltpu.VMEM((cap, QT), f32),
            pltpu.VMEM((queries, HEAD), bf),
            pltpu.VMEM((keys, HEAD), f32),
            pltpu.VMEM((keys, HEAD), f32),
            pltpu.SMEM((shards,), jnp.int32),
        ],
        compiler_params=pltpu.CompilerParams(vmem_limit_bytes=VMEM_BYTES),
        cost_estimate=pl.CostEstimate(flops=6_000_000_000, bytes_accessed=6_000_000, transcendentals=10_000_000),
        name="attention_backward",
    )(counts, place, q_own, do_own, far, *kvs)


def spread_kernel(order, target_ref, *refs):
    parts, out_ref = refs[:-1], refs[-1]
    step = pl.program_id(0)
    tokens, capacity = out_ref.shape[0], parts[0].shape[0]
    token = lax.broadcasted_iota(jnp.int32, (tokens, capacity), 0)
    pick = (token == target_ref[...]).astype(jnp.bfloat16)
    for index, part in enumerate(parts):

        @pl.when(step == index)
        def _(part=part):
            out_ref[...] = lax.dot_general(
                pick, part[...], ROWS_COLS, preferred_element_type=jnp.float32
            ).astype(jnp.bfloat16)


def spread_rows(order, target, parts, tokens):
    capacity, width = parts[0].shape
    whole = pl.BlockSpec((capacity, width), lambda s, order: (0, 0))
    return pl.pallas_call(
        spread_kernel,
        grid_spec=pltpu.PrefetchScalarGridSpec(
            num_scalar_prefetch=1,
            grid=(len(parts),),
            in_specs=[pl.BlockSpec((1, capacity), lambda s, order: (0, 0))] + [whole] * len(parts),
            out_specs=pl.BlockSpec((tokens, width), lambda s, order: (0, order[s])),
        ),
        out_shape=jax.ShapeDtypeStruct((tokens, width * len(parts)), jnp.bfloat16),
        cost_estimate=pl.CostEstimate(
            flops=800_000_000, bytes_accessed=6_000_000, transcendentals=0
        ),
        name="spread_rows",
    )(order, target[None, :], *parts)


def shards(hidden, kept, counts, queries, keys, values, out_grad, kv_weight):
    f32 = jnp.float32
    seq_devices = lax.axis_size("seq")
    dp_devices = lax.axis_size("dp")
    rep_devices = lax.axis_size("rep")
    seq_index = lax.axis_index("seq")
    dp_index = lax.axis_index("dp")
    rep_index = lax.axis_index("rep")
    capacity = queries.shape[1]
    tokens_local = hidden.shape[1]
    local_groups = keys.shape[2] // HEAD
    group_columns = queries.shape[2] // local_groups
    width = kv_weight.shape[2]
    part_rows = kv_weight.shape[0] // rep_devices
    dp_per_rep = dp_devices // rep_devices
    lane_of = (dp_index % dp_per_rep) * rep_devices + rep_index
    x_at, y_at = seq_index // SIDE, seq_index % SIDE
    group = x_at // (SIDE // local_groups)
    place = jnp.stack([x_at, y_at, group, dp_index, rep_index, lane_of]).astype(jnp.int32)
    swap = [(i, (i + 1) % rep_devices) for i in range(rep_devices)]
    mirror = [(i, (SIDE - 1 - i // SIDE) * SIDE + i % SIDE) for i in range(seq_devices)]

    def shift_dp(array, step):
        return lax.ppermute(array, "dp", [(i, (i + step) % dp_devices) for i in range(dp_devices)])

    def shift_x(array, step):
        pairs = [(i, ((i // SIDE + step) % SIDE) * SIDE + i % SIDE) for i in range(seq_devices)]
        return lax.ppermute(array, "seq", pairs)

    def shift_y(array, step):
        pairs = [(i, (i // SIDE) * SIDE + (i % SIDE + step) % SIDE) for i in range(seq_devices)]
        return lax.ppermute(array, "seq", pairs)

    by_group = [
        jnp.concatenate([keys[0][:, g * HEAD : (g + 1) * HEAD], values[0][:, g * HEAD : (g + 1) * HEAD]], axis=1)
        for g in range(local_groups)
    ]

    def pair_for(step):
        wanted = ((x_at + step) % SIDE) // (SIDE // local_groups)
        chosen = by_group[0]
        for g in range(1, local_groups):
            chosen = jnp.where(wanted == g, by_group[g], chosen)
        return chosen

    kv_x = [pair_for(0)] + [shift_x(pair_for(step), step) for step in range(1, SIDE)]
    kv_x = jnp.concatenate(kv_x, axis=0)
    sent = (1 - group) * group_columns
    far = jnp.concatenate(
        [lax.dynamic_slice_in_dim(array[0], sent, group_columns, 1) for array in (queries, out_grad)], axis=1
    )
    halves = kv_weight.reshape(rep_devices, part_rows, 2 * width)
    kept_half = lax.dynamic_index_in_dim(halves, rep_index, 0, keepdims=False)
    sent_half = lax.dynamic_index_in_dim(halves, 1 - rep_index, 0, keepdims=False)
    kv_x, far, hidden, kept_half, sent_half = lax.optimization_barrier(
        (kv_x, far, hidden, kept_half, sent_half)
    )
    kv_y = [kv_x] + [shift_y(kv_x, step) for step in range(1, SIDE)]

    far = lax.ppermute(far, "seq", mirror)

    own_rows = lax.dynamic_index_in_dim(kept[0], seq_index, 0, keepdims=False)
    own_count = lax.dynamic_index_in_dim(counts[0], seq_index, 0, keepdims=False)
    columns = gather_columns(place, own_rows, hidden[0], dp_devices, rep_devices)
    other_half = lax.ppermute(sent_half, "rep", swap)
    slot_index = jnp.arange(capacity, dtype=jnp.int32)
    target = jnp.where(slot_index < own_count, own_rows, tokens_local)
    kv_y[1:], columns, kept_half, other_half, target = lax.optimization_barrier(
        (kv_y[1:], columns, kept_half, other_half, target)
    )
    columns = lax.all_to_all(columns, "dp", split_axis=0, concat_axis=0, tiled=True)

    grads = attention_backward(counts[0], place, queries[0], out_grad[0], far, kv_y)
    (dq_own, dq_far, *kv_back), columns = lax.optimization_barrier((tuple(grads), columns))
    kv_back = [kv_back[0]] + [shift_y(kv_back[step], step) for step in range(1, SIDE)]
    dq_back = lax.ppermute(dq_far, "seq", mirror)
    columns_far = lax.ppermute(columns, "rep", swap)
    kv_back[-1], columns_far = lax.optimization_barrier((kv_back[-1], columns_far))

    pieces = y_sum(place, kv_back)
    pieces = [pieces[0]] + [shift_x(pieces[step], step) for step in range(1, SIDE)]
    pieces, dq_back = lax.optimization_barrier((pieces, dq_back))
    kv_grad = x_sum(place, pieces, local_groups)
    dq_first = jnp.where(group == 0, dq_own, dq_back)
    dq_last = jnp.where(group == 0, dq_back, dq_own)
    back_query = jnp.concatenate([dq_first, dq_last], axis=1)

    kv_all = [kv_grad] + [shift_dp(kv_grad, step) for step in range(1, dp_devices)]
    kv_far = [lax.ppermute(part, "rep", swap) for part in kv_all]
    kv_all, kv_far[:-1], back_query = lax.optimization_barrier((kv_all, kv_far[:-1], back_query))

    terms = weight_terms(place, columns, columns_far, kv_all)
    terms = lax.all_to_all(
        terms.reshape(seq_devices, -1, 2 * width), "seq", split_axis=0, concat_axis=0, tiled=True
    )
    grad_weight = jnp.sum(terms.astype(f32), axis=0).reshape(-1, 2, width)

    products = input_products(place, kv_all, kv_far, kept_half, other_half)
    received = []
    for step in range(dp_devices):
        pairs = []
        for dp in range(dp_devices):
            for rep in range(rep_devices):
                lane = (dp % dp_per_rep) * rep_devices + rep
                to_dp = (lane + step) % dp_devices
                pairs.append((dp * rep_devices + rep, to_dp * rep_devices + dp // dp_per_rep))
        received.append(lax.ppermute(products[step], ("dp", "rep"), pairs))
    order = jnp.stack([(dp_index - step) % dp_devices for step in range(dp_devices)]).astype(jnp.int32)
    grad_hidden = spread_rows(order, target, received, tokens_local)
    return (back_query[None], grad_hidden[None], grad_weight)


def solution(mesh):
    placed = (
        P("dp", "seq", None),
        P("dp", None, None),
        P("dp", None),
        P("dp", "seq", "rep"),
        P("dp", "seq", "rep"),
        P("dp", "seq", "rep"),
        P("dp", "seq", "rep"),
        P("dp", None, "rep"),
    )
    return jax.shard_map(
        shards,
        mesh=mesh,
        in_specs=placed,
        out_specs=(P("dp", "seq", "rep"), P("dp", "seq", "rep"), P(("seq", "dp"), None, "rep")),
        check_vma=False,
    )
```

```python
import functools

import jax
import jax.numpy as jnp
from jax import lax
from jax.experimental import pallas as pl
from jax.experimental.pallas import tpu as pltpu
from jax.sharding import PartitionSpec as P

HEAD = 128
MASKED = -1e30
LOG2E = 1.4426950408889634
ROWS_ROWS = (((1,), (1,)), ((), ()))
ROWS_COLS = (((1,), (0,)), ((), ()))
QT = 512
KT = 512
VMEM_BYTES = 56 * 1024 * 1024
SIDE = 4


def gather_kernel(place, rows_ref, hidden_ref, out_ref, pick_ref):
    capacity, tokens = rows_ref.shape[0], hidden_ref.shape[0]

    @pl.when(pl.program_id(0) == 0)
    def _():
        token = lax.broadcasted_iota(jnp.int32, (capacity, tokens), 1)
        pick_ref[...] = (token == rows_ref[...]).astype(jnp.bfloat16)

    picked = lax.dot_general(
        pick_ref[...], hidden_ref[...], ROWS_COLS, preferred_element_type=jnp.float32
    ).astype(jnp.bfloat16)
    parts = out_ref.shape[0]
    for part in range(parts):
        for block in range(out_ref.shape[2] // HEAD):
            first = (block * parts + part) * HEAD
            out_ref[part, :, block * HEAD : (block + 1) * HEAD] = picked[:, first : first + HEAD]


def gather_columns(place, rows, hidden, parts, cores):
    capacity = rows.shape[0]
    tokens, width = hidden.shape
    half = width // cores
    steps = 4
    block = half // steps
    return pl.pallas_call(
        gather_kernel,
        grid_spec=pltpu.PrefetchScalarGridSpec(
            num_scalar_prefetch=1,
            grid=(steps,),
            in_specs=[
                pl.BlockSpec((capacity, 1), lambda s, place: (0, 0)),
                pl.BlockSpec((tokens, block), lambda s, place: (0, place[4] * steps + s)),
            ],
            out_specs=pl.BlockSpec((parts, capacity, block // parts), lambda s, place: (0, 0, s)),
            scratch_shapes=[pltpu.VMEM((capacity, tokens), jnp.bfloat16)],
        ),
        out_shape=jax.ShapeDtypeStruct((parts, capacity, half // parts), hidden.dtype),
        cost_estimate=pl.CostEstimate(
            flops=800_000_000, bytes_accessed=6_000_000, transcendentals=0
        ),
        name="gather_columns",
    )(place, rows[:, None], hidden)


def y_sum_kernel(place, *refs):
    parts, outs = refs[:4], refs[4:]
    cap = outs[0].shape[0]
    for step, out in enumerate(outs):
        at = pl.ds(pl.multiple_of(((place[0] + step) % len(outs)) * cap, 64), cap)
        total = parts[0][at, :].astype(jnp.float32)
        for part in parts[1:]:
            total = total + part[at, :].astype(jnp.float32)
        out[...] = total.astype(jnp.bfloat16)


def y_sum(place, parts):
    rows, width = parts[0].shape
    vmem = pl.BlockSpec(memory_space=pltpu.VMEM)
    return pl.pallas_call(
        y_sum_kernel,
        in_specs=[pl.BlockSpec(memory_space=pltpu.SMEM)] + [vmem] * len(parts),
        out_specs=[vmem] * len(parts),
        out_shape=[jax.ShapeDtypeStruct((rows // len(parts), width), jnp.bfloat16)] * len(parts),
        cost_estimate=pl.CostEstimate(
            flops=1_000_000, bytes_accessed=2_000_000, transcendentals=0
        ),
        name="y_sum",
    )(place, *parts)


def x_sum_kernel(place, *refs):
    parts, out_ref, by_x = refs[:-2], refs[-2], refs[-1]
    cap = out_ref.shape[0]
    count = len(parts)
    groups = out_ref.shape[1] // (2 * HEAD)
    for step, part in enumerate(parts):
        at = pl.ds(pl.multiple_of(((place[0] - step) % count) * cap, 64), cap)
        by_x[at, :] = part[...].astype(jnp.float32)
    size = count // groups
    for group in range(groups):
        total = by_x[group * size * cap : (group * size + 1) * cap, :]
        for x in range(group * size + 1, (group + 1) * size):
            total = total + by_x[x * cap : (x + 1) * cap, :]
        total = total.astype(jnp.bfloat16)
        for kind in range(2):
            first = (kind * groups + group) * HEAD
            out_ref[:, first : first + HEAD] = total[:, kind * HEAD : (kind + 1) * HEAD]


def x_sum(place, parts, groups):
    rows, width = parts[0].shape
    vmem = pl.BlockSpec(memory_space=pltpu.VMEM)
    return pl.pallas_call(
        x_sum_kernel,
        in_specs=[pl.BlockSpec(memory_space=pltpu.SMEM)] + [vmem] * len(parts),
        out_specs=vmem,
        out_shape=jax.ShapeDtypeStruct((rows, groups * width), jnp.bfloat16),
        scratch_shapes=[pltpu.VMEM((rows * len(parts), width), jnp.float32)],
        cost_estimate=pl.CostEstimate(
            flops=1_000_000, bytes_accessed=1_000_000, transcendentals=0
        ),
        name="x_sum",
    )(place, *parts)


def terms_kernel(place, own_ref, other_ref, *refs):
    kv, (out_ref, columns_s, kv_s) = refs[:-3], refs[-3:]
    count, cap = len(kv), kv[0].shape[0]
    step = pl.program_id(0)

    def collect(columns_ref):
        for index in range(count):
            held = (place[3] - index) % count
            columns_s[index * cap : (index + 1) * cap, :] = columns_ref[held]

    @pl.when(step == 0)
    def _():
        collect(own_ref)
        for index, part in enumerate(kv):
            kv_s[index * cap : (index + 1) * cap, :] = part[...]

    @pl.when(step == 1)
    def _():
        collect(other_ref)

    out_ref[...] = lax.dot_general(
        columns_s[...], kv_s[...], (((0,), (0,)), ((), ())), preferred_element_type=jnp.float32
    ).astype(jnp.bfloat16)


def weight_terms(place, own, other, kv):
    count, cap, half = own.shape
    width = kv[0].shape[1]
    columns = pl.BlockSpec((count, cap, half), lambda s, place: (0, 0, 0))
    return pl.pallas_call(
        terms_kernel,
        grid_spec=pltpu.PrefetchScalarGridSpec(
            num_scalar_prefetch=1,
            grid=(2,),
            in_specs=[columns] * 2
            + [pl.BlockSpec((cap, width), lambda s, place: (0, 0))] * len(kv),
            out_specs=pl.BlockSpec((half, width), lambda s, place: ((s + place[4]) % 2, 0)),
            scratch_shapes=[
                pltpu.VMEM((count * cap, half), jnp.bfloat16),
                pltpu.VMEM((count * cap, width), jnp.bfloat16),
            ],
        ),
        out_shape=jax.ShapeDtypeStruct((2 * half, width), jnp.bfloat16),
        compiler_params=pltpu.CompilerParams(vmem_limit_bytes=VMEM_BYTES),
        cost_estimate=pl.CostEstimate(
            flops=1_600_000_000, bytes_accessed=6_000_000, transcendentals=0
        ),
        name="weight_terms",
    )(place, own, other, *kv)


def products_kernel(place, *refs):
    w_own, w_other, out_s, kv_s = refs[-4:]
    count = (len(refs) - 4) // 3
    own, other, parts = refs[:count], refs[count : 2 * count], refs[2 * count : 3 * count]
    cap, half = own[0].shape
    for index in range(count):
        kv_s[index * cap : (index + 1) * cap, :half] = own[index][...]
        kv_s[index * cap : (index + 1) * cap, half:] = other[index][...]
    chunk = 512
    for first in range(0, out_s.shape[1], chunk):
        here = slice(first, first + chunk)
        total = lax.dot_general(
            kv_s[:, :half], w_own[here, :], ROWS_ROWS, preferred_element_type=jnp.float32
        ) + lax.dot_general(
            kv_s[:, half:], w_other[here, :], ROWS_ROWS, preferred_element_type=jnp.float32
        )
        out_s[:, here] = total.astype(jnp.bfloat16)
    for step, part in enumerate(parts):
        held = (place[3] - place[5] - step) % count
        part[...] = out_s[pl.ds(pl.multiple_of(held * cap, 64), cap), :]


def input_products(place, own, other, w_own, w_other):
    cap, half = own[0].shape
    count, width = len(own), w_own.shape[0]
    vmem = pl.BlockSpec(memory_space=pltpu.VMEM)

    def body(place, *refs):
        ins, outs, scratch = refs[: 2 * count + 2], refs[2 * count + 2 : 3 * count + 2], refs[3 * count + 2 :]
        products_kernel(place, *ins[: 2 * count], *outs, ins[-2], ins[-1], *scratch)

    return pl.pallas_call(
        body,
        in_specs=[pl.BlockSpec(memory_space=pltpu.SMEM)] + [vmem] * (2 * count + 2),
        out_specs=[vmem] * count,
        out_shape=[jax.ShapeDtypeStruct((cap, width), jnp.bfloat16)] * count,
        scratch_shapes=[
            pltpu.VMEM((count * cap, width), jnp.bfloat16),
            pltpu.VMEM((count * cap, 2 * half), jnp.bfloat16),
        ],
        compiler_params=pltpu.CompilerParams(vmem_limit_bytes=VMEM_BYTES),
        cost_estimate=pl.CostEstimate(
            flops=1_600_000_000, bytes_accessed=6_000_000, transcendentals=0
        ),
        name="input_products",
    )(place, *own, *other, w_own, w_other)


def attention_kernel(counts, place, q_own, do_own, far, kv0, kv1, kv2, kv3,
                     dq_own, dq_far, out0, out1, out2, out3,
                     kv_s, k_s, kt_s, v_s, q_s, do_s, tri_s, s_s, g_s, so_s, go_s, dq_s, dk_s, dv_s, off_s):
    bf, f32 = jnp.bfloat16, jnp.float32
    cap = q_own.shape[0]
    far_heads = far.shape[1] // (2 * HEAD)
    shards = counts.shape[0]
    side = 4
    scale = HEAD**-0.5
    x_at, y_at, group = place[0], place[1], place[2]
    row = lax.broadcasted_iota(jnp.int32, (cap, HEAD), 0)
    lane = lax.broadcasted_iota(jnp.int32, (cap, HEAD), 1)
    zero = jnp.zeros((cap, HEAD), bf)

    def up16(value):
        return ((value + 15) // 16) * 16

    block = side * cap
    for index, ref in enumerate((kv0, kv1, kv2, kv3)):
        kv_s[index * block : (index + 1) * block, :] = ref[...]
    total = jnp.int32(0)
    for s in range(shards):
        off_s[s] = total
        at = pl.ds(pl.multiple_of(total, 16), cap)
        held = ((y_at - s % side) % side) * side + (x_at - s // side) % side
        pair = kv_s[pl.ds(pl.multiple_of(held * cap, 64), cap), :]
        live = row < counts[s]
        k_s[at, :HEAD] = jnp.where(live, pair[:, :HEAD], zero)
        k_s[at, HEAD:] = jnp.where(live, 0.0, jnp.where(lane == 0, MASKED, 0.0)).astype(bf)
        v_s[at, :] = jnp.where(live, pair[:, HEAD:], zero)
        total = total + up16(counts[s])
    end = pl.ds(pl.multiple_of(total, 16), KT)
    k_s[end, :HEAD] = jnp.zeros((KT, HEAD), bf)
    k_s[end, HEAD:] = jnp.zeros((KT, HEAD), bf)
    v_s[end, :] = jnp.zeros((KT, HEAD), bf)

    def k_at(index):
        return pl.ds(pl.multiple_of(index * KT, KT), KT)

    def prepare(j, carry):
        at = k_at(j)
        kt_s[:, at] = k_s[at, :HEAD].T
        dk_s[at, :] = jnp.zeros((KT, HEAD), f32)
        dv_s[at, :] = jnp.zeros((KT, HEAD), f32)
        return carry

    lax.fori_loop(0, (total + cap + KT - 1) // KT, prepare, 0)
    one_lane = lax.broadcasted_iota(jnp.int32, (QT, HEAD), 1)
    ones = jnp.where(one_lane == 0, 1.0, 0.0).astype(bf)
    slot = lax.broadcasted_iota(jnp.int32, (cap, 2 * HEAD), 0)
    key_slot = lax.broadcasted_iota(jnp.int32, (cap, 2 * HEAD), 1)
    later = jnp.where(key_slot > slot, MASKED, 0.0).astype(bf)
    same = jnp.where(key_slot == slot, 1.0, 0.0).astype(bf)
    key_row = lax.broadcasted_iota(jnp.int32, (KT, QT), 0)

    def one_shard(shard, q_ref, do_ref, q_first, do_first, dq_ref):
        count = counts[shard]
        before = pl.multiple_of(off_s[shard], 16)
        rows = up16(count)
        live = row < count
        for h in range(far_heads):
            at = pl.ds(pl.multiple_of(h * rows, 16), cap)
            q_here = pl.ds(pl.multiple_of(q_first + h * HEAD, HEAD), HEAD)
            do_here = pl.ds(pl.multiple_of(do_first + h * HEAD, HEAD), HEAD)
            q_s[at, :] = jnp.where(live, q_ref[:, q_here], zero)
            do_s[at, :] = jnp.where(live, do_ref[:, do_here], zero)
            tri_s[at, :] = later
        tail = pl.ds(pl.multiple_of(far_heads * rows, 16), QT)
        q_s[tail, :] = jnp.zeros((QT, HEAD), bf)
        do_s[tail, :] = jnp.zeros((QT, HEAD), bf)
        tri_s[tail, :] = jnp.zeros((QT, 2 * HEAD), bf)
        own = pl.ds(before, cap)
        full = before // KT
        rest = before - full * KT
        tiles = (far_heads * rows + QT - 1) // QT

        def query_step(i, carry):
            q_at = pl.ds(pl.multiple_of(i * QT, QT), QT)
            q = q_s[q_at, :]
            do = do_s[q_at, :]
            q_one = jnp.concatenate([q, ones], axis=1)
            own_k = k_s[own, :HEAD]
            scores = lax.dot_general(own_k, q, ROWS_ROWS, preferred_element_type=f32) * (scale * LOG2E)
            scores = scores + lax.dot_general(same, tri_s[q_at, :], ROWS_ROWS, preferred_element_type=f32)
            grads = lax.dot_general(v_s[own, :], do, ROWS_ROWS, preferred_element_type=f32)
            so_s[...] = scores
            go_s[...] = grads
            high = jnp.max(scores, axis=0, keepdims=True)
            e = jnp.exp2(scores - high)
            state = (high, jnp.sum(e, axis=0, keepdims=True), jnp.sum(e * grads, axis=0, keepdims=True))

            def scan(j, state, partial):
                high, total_e, total_w = state
                at = k_at(j)
                scores = lax.dot_general(k_s[at, :], q_one, ROWS_ROWS, preferred_element_type=f32)
                grads = lax.dot_general(v_s[at, :], do, ROWS_ROWS, preferred_element_type=f32)
                scores = scores * (scale * LOG2E)
                if partial:
                    scores = jnp.where(key_row < rest, scores, MASKED)
                s_s[at, :] = scores
                g_s[at, :] = grads
                new = jnp.maximum(high, jnp.max(scores, axis=0, keepdims=True))
                e = jnp.exp2(scores - new)
                shrink = jnp.exp2(high - new)
                return (
                    new,
                    total_e * shrink + jnp.sum(e, axis=0, keepdims=True),
                    total_w * shrink + jnp.sum(e * grads, axis=0, keepdims=True),
                )

            state = lax.fori_loop(0, full, functools.partial(scan, partial=False), state)
            ends = full + (rest > 0).astype(jnp.int32)
            high, total_e, total_w = lax.fori_loop(full, ends, functools.partial(scan, partial=True), state)
            delta = total_w / total_e
            log_total = high + jnp.log2(total_e)

            def spread(at, key_t, scores, grads):
                probs = jnp.exp2(scores - log_total)
                dscore = (probs * (grads - delta)).astype(bf)
                dv_s[at, :] += lax.dot_general(probs.astype(bf), do, ROWS_COLS, preferred_element_type=f32)
                dk_s[at, :] += lax.dot_general(dscore, q, ROWS_COLS, preferred_element_type=f32)
                return lax.dot_general(key_t, dscore, ROWS_COLS, preferred_element_type=f32)

            dq = spread(own, own_k.T, so_s[...], go_s[...])
            dq = lax.fori_loop(
                0, ends, lambda j, dq: dq + spread(k_at(j), kt_s[:, k_at(j)], s_s[k_at(j), :], g_s[k_at(j), :]), dq
            )
            dq_s[q_at, :] = (dq * scale).T.astype(bf)
            return carry

        lax.fori_loop(0, tiles, query_step, 0)
        for h in range(far_heads):
            at = pl.ds(pl.multiple_of(h * rows, 16), cap)
            dq_ref[:, h * HEAD : (h + 1) * HEAD] = jnp.where(live, dq_s[at, :], zero)

    span = far_heads * HEAD
    one_shard(x_at * side + y_at, q_own, do_own, group * span, group * span, dq_own)
    one_shard((side - 1 - x_at) * side + y_at, far, far, 0, span, dq_far)

    for step, ref in enumerate((out0, out1, out2, out3)):
        for x in range(side):
            shard = x * side + (y_at + step) % side
            at = pl.ds(pl.multiple_of(off_s[shard], 16), cap)
            here = slice(x * cap, (x + 1) * cap)
            live = row < counts[shard]
            ref[here, :HEAD] = jnp.where(live, dk_s[at, :] * scale, 0.0).astype(bf)
            ref[here, HEAD:] = jnp.where(live, dv_s[at, :], 0.0).astype(bf)


def attention_backward(counts, place, q_own, do_own, far, kvs):
    cap, width = far.shape[0], far.shape[1] // 2
    shards = counts.shape[0]
    rows = shards * cap
    keys = -(-(rows + KT) // KT) * KT
    queries = -(-(cap * (width // HEAD) + max(QT, cap)) // QT) * QT
    bf, f32 = jnp.bfloat16, jnp.float32
    vmem = pl.BlockSpec(memory_space=pltpu.VMEM)
    smem = pl.BlockSpec(memory_space=pltpu.SMEM)
    block = kvs[0].shape
    return pl.pallas_call(
        attention_kernel,
        out_shape=[jax.ShapeDtypeStruct((cap, width), bf)] * 2 + [jax.ShapeDtypeStruct(block, bf)] * 4,
        in_specs=[smem, smem] + [vmem] * 7,
        out_specs=[vmem] * 6,
        scratch_shapes=[
            pltpu.VMEM((rows, 2 * HEAD), bf),
            pltpu.VMEM((keys, 2 * HEAD), bf),
            pltpu.VMEM((HEAD, keys), bf),
            pltpu.VMEM((keys, HEAD), bf),
            pltpu.VMEM((queries, HEAD), bf),
            pltpu.VMEM((queries, HEAD), bf),
            pltpu.VMEM((queries, 2 * HEAD), bf),
            pltpu.VMEM((keys, QT), f32),
            pltpu.VMEM((keys, QT), f32),
            pltpu.VMEM((cap, QT), f32),
            pltpu.VMEM((cap, QT), f32),
            pltpu.VMEM((queries, HEAD), bf),
            pltpu.VMEM((keys, HEAD), f32),
            pltpu.VMEM((keys, HEAD), f32),
            pltpu.SMEM((shards,), jnp.int32),
        ],
        compiler_params=pltpu.CompilerParams(vmem_limit_bytes=VMEM_BYTES),
        cost_estimate=pl.CostEstimate(flops=6_000_000_000, bytes_accessed=6_000_000, transcendentals=10_000_000),
        name="attention_backward",
    )(counts, place, q_own, do_own, far, *kvs)


def spread_kernel(order, target_ref, *refs):
    parts, (out_ref, pick_ref) = refs[:2], refs[-2:]
    step = pl.program_id(0)
    tokens, capacity = pick_ref.shape

    @pl.when(step == 0)
    def _():
        token = lax.broadcasted_iota(jnp.int32, (tokens, capacity), 0)
        pick_ref[...] = (token == target_ref[...]).astype(jnp.bfloat16)

    for index, part in enumerate(parts):

        @pl.when(step == index)
        def _(part=part):
            out_ref[...] = lax.dot_general(
                pick_ref[...], part[...], ROWS_COLS, preferred_element_type=jnp.float32
            ).astype(jnp.bfloat16)


def spread_rows(order, target, parts, shape, held=()):
    capacity, width = parts[0].shape
    tokens = shape[0]
    whole = pl.BlockSpec((capacity, width), lambda s, order: (0, 0))
    return pl.pallas_call(
        spread_kernel,
        grid_spec=pltpu.PrefetchScalarGridSpec(
            num_scalar_prefetch=1,
            grid=(len(parts),),
            in_specs=[pl.BlockSpec((1, capacity), lambda s, order: (0, 0))]
            + [whole] * len(parts)
            + [pl.BlockSpec(memory_space=pl.ANY)] * len(held),
            out_specs=pl.BlockSpec((tokens, width), lambda s, order: (0, order[s])),
            scratch_shapes=[pltpu.VMEM((tokens, capacity), jnp.bfloat16)],
        ),
        out_shape=jax.ShapeDtypeStruct(shape, jnp.bfloat16),
        input_output_aliases={2 + len(parts): 0} if held else {},
        cost_estimate=pl.CostEstimate(
            flops=400_000_000, bytes_accessed=3_000_000, transcendentals=0
        ),
        name="spread_rows",
    )(order, target[None, :], *parts, *held)


def shards(hidden, kept, counts, queries, keys, values, out_grad, kv_weight):
    f32 = jnp.float32
    seq_devices = lax.axis_size("seq")
    dp_devices = lax.axis_size("dp")
    rep_devices = lax.axis_size("rep")
    seq_index = lax.axis_index("seq")
    dp_index = lax.axis_index("dp")
    rep_index = lax.axis_index("rep")
    capacity = queries.shape[1]
    tokens_local = hidden.shape[1]
    local_groups = keys.shape[2] // HEAD
    group_columns = queries.shape[2] // local_groups
    width = kv_weight.shape[2]
    part_rows = kv_weight.shape[0] // rep_devices
    dp_per_rep = dp_devices // rep_devices
    lane_of = (dp_index % dp_per_rep) * rep_devices + rep_index
    x_at, y_at = seq_index // SIDE, seq_index % SIDE
    group = x_at // (SIDE // local_groups)
    place = jnp.stack([x_at, y_at, group, dp_index, rep_index, lane_of]).astype(jnp.int32)
    swap = [(i, (i + 1) % rep_devices) for i in range(rep_devices)]
    mirror = [(i, (SIDE - 1 - i // SIDE) * SIDE + i % SIDE) for i in range(seq_devices)]

    def shift_dp(array, step):
        return lax.ppermute(array, "dp", [(i, (i + step) % dp_devices) for i in range(dp_devices)])

    def shift_x(array, step):
        pairs = [(i, ((i // SIDE + step) % SIDE) * SIDE + i % SIDE) for i in range(seq_devices)]
        return lax.ppermute(array, "seq", pairs)

    def shift_y(array, step):
        pairs = [(i, (i // SIDE) * SIDE + (i % SIDE + step) % SIDE) for i in range(seq_devices)]
        return lax.ppermute(array, "seq", pairs)

    by_group = [
        jnp.concatenate([keys[0][:, g * HEAD : (g + 1) * HEAD], values[0][:, g * HEAD : (g + 1) * HEAD]], axis=1)
        for g in range(local_groups)
    ]

    def pair_for(step):
        wanted = ((x_at + step) % SIDE) // (SIDE // local_groups)
        chosen = by_group[0]
        for g in range(1, local_groups):
            chosen = jnp.where(wanted == g, by_group[g], chosen)
        return chosen

    kv_x = [pair_for(0)] + [shift_x(pair_for(step), step) for step in range(1, SIDE)]
    kv_x = jnp.concatenate(kv_x, axis=0)
    sent = (1 - group) * group_columns
    far = jnp.concatenate(
        [lax.dynamic_slice_in_dim(array[0], sent, group_columns, 1) for array in (queries, out_grad)], axis=1
    )
    kv_x, far, hidden = lax.optimization_barrier((kv_x, far, hidden))
    kv_y = [kv_x] + [shift_y(kv_x, step) for step in range(1, SIDE)]

    far = lax.ppermute(far, "seq", mirror)

    own_rows = lax.dynamic_index_in_dim(kept[0], seq_index, 0, keepdims=False)
    own_count = lax.dynamic_index_in_dim(counts[0], seq_index, 0, keepdims=False)
    columns = gather_columns(place, own_rows, hidden[0], dp_devices, rep_devices)
    slot_index = jnp.arange(capacity, dtype=jnp.int32)
    target = jnp.where(slot_index < own_count, own_rows, tokens_local)
    kv_y[1:], columns, target = lax.optimization_barrier((kv_y[1:], columns, target))
    columns = lax.all_to_all(columns, "dp", split_axis=0, concat_axis=0, tiled=True)

    grads = attention_backward(counts[0], place, queries[0], out_grad[0], far, kv_y)
    (dq_own, dq_far, *kv_back), columns = lax.optimization_barrier((tuple(grads), columns))
    kv_back = [kv_back[0]] + [shift_y(kv_back[step], step) for step in range(1, SIDE)]
    dq_back = lax.ppermute(dq_far, "seq", mirror)
    columns_far = lax.ppermute(columns, "rep", swap)
    dq_back, kv_weight = lax.optimization_barrier((dq_back, kv_weight))
    halves = kv_weight.reshape(rep_devices, part_rows, 2 * width)
    kept_half = lax.dynamic_index_in_dim(halves, rep_index, 0, keepdims=False)
    sent_half = lax.dynamic_index_in_dim(halves, 1 - rep_index, 0, keepdims=False)
    kv_back[-1], columns_far, kept_half, sent_half = lax.optimization_barrier(
        (kv_back[-1], columns_far, kept_half, sent_half)
    )

    pieces = y_sum(place, kv_back)
    pieces, sent_half = lax.optimization_barrier((pieces, sent_half))
    other_half = lax.ppermute(sent_half, "rep", swap)
    pieces = [pieces[0]] + [shift_x(pieces[step], step) for step in range(1, SIDE)]
    pieces, dq_back, other_half = lax.optimization_barrier((pieces, dq_back, other_half))
    kv_grad = x_sum(place, pieces, local_groups)
    dq_first = jnp.where(group == 0, dq_own, dq_back)
    dq_last = jnp.where(group == 0, dq_back, dq_own)
    back_query = jnp.concatenate([dq_first, dq_last], axis=1)

    kv_all = [kv_grad] + [shift_dp(kv_grad, step) for step in range(1, dp_devices)]
    kv_far = [lax.ppermute(part, "rep", swap) for part in kv_all]
    kv_all, kv_far, back_query = lax.optimization_barrier((kv_all, kv_far, back_query))

    terms = weight_terms(place, columns, columns_far, kv_all)
    terms = lax.all_to_all(
        terms.reshape(seq_devices, -1, 2 * width), "seq", split_axis=0, concat_axis=0, tiled=True
    )
    grad_weight = jnp.sum(terms.astype(f32), axis=0).reshape(-1, 2, width)

    products = input_products(place, kv_all, kv_far, kept_half, other_half)
    received = []
    for step in range(dp_devices):
        pairs = []
        for dp in range(dp_devices):
            for rep in range(rep_devices):
                lane = (dp % dp_per_rep) * rep_devices + rep
                to_dp = (lane + step) % dp_devices
                pairs.append((dp * rep_devices + rep, to_dp * rep_devices + dp // dp_per_rep))
        received.append(lax.ppermute(products[step], ("dp", "rep"), pairs))
    held = ()
    for steps in ((0, 3), (1, 2)):
        order = jnp.stack([(dp_index - step) % dp_devices for step in steps]).astype(jnp.int32)
        parts = [received[step] for step in steps]
        held = (spread_rows(order, target, parts, (tokens_local, dp_devices * part_rows), held),)
    grad_hidden = held[0]
    return (back_query[None], grad_hidden[None], grad_weight)


def solution(mesh):
    placed = (
        P("dp", "seq", None),
        P("dp", None, None),
        P("dp", None),
        P("dp", "seq", "rep"),
        P("dp", "seq", "rep"),
        P("dp", "seq", "rep"),
        P("dp", "seq", "rep"),
        P("dp", None, "rep"),
    )
    return jax.shard_map(
        shards,
        mesh=mesh,
        in_specs=placed,
        out_specs=(P("dp", "seq", "rep"), P("dp", "seq", "rep"), P(("seq", "dp"), None, "rep")),
        check_vma=False,
    )
```

```python
import functools

import jax
import jax.numpy as jnp
from jax import lax
from jax.experimental import pallas as pl
from jax.experimental.pallas import tpu as pltpu
from jax.sharding import PartitionSpec as P

HEAD = 128
MASKED = -1e30
LOG2E = 1.4426950408889634
ROWS_ROWS = (((1,), (1,)), ((), ()))
ROWS_COLS = (((1,), (0,)), ((), ()))
QT = 512
WIDE = 1024
KT = 512
VMEM_BYTES = 56 * 1024 * 1024
SIDE = 4


def gather_kernel(place, rows_ref, hidden_ref, out_ref, pick_ref):
    capacity, tokens = rows_ref.shape[0], hidden_ref.shape[0]

    @pl.when(pl.program_id(0) == 0)
    def _():
        token = lax.broadcasted_iota(jnp.int32, (capacity, tokens), 1)
        pick_ref[...] = (token == rows_ref[...]).astype(jnp.bfloat16)

    picked = lax.dot_general(
        pick_ref[...], hidden_ref[...], ROWS_COLS, preferred_element_type=jnp.float32
    ).astype(jnp.bfloat16)
    parts = out_ref.shape[0]
    for part in range(parts):
        for block in range(out_ref.shape[2] // HEAD):
            first = (block * parts + part) * HEAD
            out_ref[part, :, block * HEAD : (block + 1) * HEAD] = picked[:, first : first + HEAD]


def gather_columns(place, rows, hidden, parts, cores):
    capacity = rows.shape[0]
    tokens, width = hidden.shape
    half = width // cores
    steps = 4
    block = half // steps
    return pl.pallas_call(
        gather_kernel,
        grid_spec=pltpu.PrefetchScalarGridSpec(
            num_scalar_prefetch=1,
            grid=(steps,),
            in_specs=[
                pl.BlockSpec((capacity, 1), lambda s, place: (0, 0)),
                pl.BlockSpec((tokens, block), lambda s, place: (0, place[4] * steps + s)),
            ],
            out_specs=pl.BlockSpec((parts, capacity, block // parts), lambda s, place: (0, 0, s)),
            scratch_shapes=[pltpu.VMEM((capacity, tokens), jnp.bfloat16)],
        ),
        out_shape=jax.ShapeDtypeStruct((parts, capacity, half // parts), hidden.dtype),
        cost_estimate=pl.CostEstimate(
            flops=800_000_000, bytes_accessed=6_000_000, transcendentals=0
        ),
        name="gather_columns",
    )(place, rows[:, None], hidden)


def y_sum_kernel(place, *refs):
    parts, outs = refs[:4], refs[4:]
    cap = outs[0].shape[0]
    for step, out in enumerate(outs):
        at = pl.ds(pl.multiple_of(((place[0] + step) % len(outs)) * cap, 64), cap)
        total = parts[0][at, :].astype(jnp.float32)
        for part in parts[1:]:
            total = total + part[at, :].astype(jnp.float32)
        out[...] = total.astype(jnp.bfloat16)


def y_sum(place, parts):
    rows, width = parts[0].shape
    vmem = pl.BlockSpec(memory_space=pltpu.VMEM)
    return pl.pallas_call(
        y_sum_kernel,
        in_specs=[pl.BlockSpec(memory_space=pltpu.SMEM)] + [vmem] * len(parts),
        out_specs=[vmem] * len(parts),
        out_shape=[jax.ShapeDtypeStruct((rows // len(parts), width), jnp.bfloat16)] * len(parts),
        cost_estimate=pl.CostEstimate(
            flops=1_000_000, bytes_accessed=2_000_000, transcendentals=0
        ),
        name="y_sum",
    )(place, *parts)


def x_sum_kernel(place, *refs):
    parts, out_ref, by_x = refs[:-2], refs[-2], refs[-1]
    cap = out_ref.shape[0]
    count = len(parts)
    groups = out_ref.shape[1] // (2 * HEAD)
    for step, part in enumerate(parts):
        at = pl.ds(pl.multiple_of(((place[0] - step) % count) * cap, 64), cap)
        by_x[at, :] = part[...].astype(jnp.float32)
    size = count // groups
    for group in range(groups):
        total = by_x[group * size * cap : (group * size + 1) * cap, :]
        for x in range(group * size + 1, (group + 1) * size):
            total = total + by_x[x * cap : (x + 1) * cap, :]
        total = total.astype(jnp.bfloat16)
        for kind in range(2):
            first = (kind * groups + group) * HEAD
            out_ref[:, first : first + HEAD] = total[:, kind * HEAD : (kind + 1) * HEAD]


def x_sum(place, parts, groups):
    rows, width = parts[0].shape
    vmem = pl.BlockSpec(memory_space=pltpu.VMEM)
    return pl.pallas_call(
        x_sum_kernel,
        in_specs=[pl.BlockSpec(memory_space=pltpu.SMEM)] + [vmem] * len(parts),
        out_specs=vmem,
        out_shape=jax.ShapeDtypeStruct((rows, groups * width), jnp.bfloat16),
        scratch_shapes=[pltpu.VMEM((rows * len(parts), width), jnp.float32)],
        cost_estimate=pl.CostEstimate(
            flops=1_000_000, bytes_accessed=1_000_000, transcendentals=0
        ),
        name="x_sum",
    )(place, *parts)


def terms_kernel(place, own_ref, other_ref, *refs):
    kv, (out_ref, columns_s, kv_s) = refs[:-3], refs[-3:]
    count, cap = len(kv), kv[0].shape[0]
    step = pl.program_id(0)

    def collect(columns_ref):
        for index in range(count):
            held = (place[3] - index) % count
            columns_s[index * cap : (index + 1) * cap, :] = columns_ref[held]

    @pl.when(step == 0)
    def _():
        collect(own_ref)
        for index, part in enumerate(kv):
            kv_s[index * cap : (index + 1) * cap, :] = part[...]

    @pl.when(step == 1)
    def _():
        collect(other_ref)

    out_ref[...] = lax.dot_general(
        columns_s[...], kv_s[...], (((0,), (0,)), ((), ())), preferred_element_type=jnp.float32
    ).astype(jnp.bfloat16)


def weight_terms(place, own, other, kv):
    count, cap, half = own.shape
    width = kv[0].shape[1]
    columns = pl.BlockSpec((count, cap, half), lambda s, place: (0, 0, 0))
    return pl.pallas_call(
        terms_kernel,
        grid_spec=pltpu.PrefetchScalarGridSpec(
            num_scalar_prefetch=1,
            grid=(2,),
            in_specs=[columns] * 2
            + [pl.BlockSpec((cap, width), lambda s, place: (0, 0))] * len(kv),
            out_specs=pl.BlockSpec((half, width), lambda s, place: ((s + place[4]) % 2, 0)),
            scratch_shapes=[
                pltpu.VMEM((count * cap, half), jnp.bfloat16),
                pltpu.VMEM((count * cap, width), jnp.bfloat16),
            ],
        ),
        out_shape=jax.ShapeDtypeStruct((2 * half, width), jnp.bfloat16),
        compiler_params=pltpu.CompilerParams(vmem_limit_bytes=VMEM_BYTES),
        cost_estimate=pl.CostEstimate(
            flops=1_600_000_000, bytes_accessed=6_000_000, transcendentals=0
        ),
        name="weight_terms",
    )(place, own, other, *kv)


def products_kernel(place, *refs):
    w_own, w_other, out_s, kv_s = refs[-4:]
    count = (len(refs) - 4) // 3
    own, other, parts = refs[:count], refs[count : 2 * count], refs[2 * count : 3 * count]
    cap, half = own[0].shape
    for index in range(count):
        kv_s[index * cap : (index + 1) * cap, :half] = own[index][...]
        kv_s[index * cap : (index + 1) * cap, half:] = other[index][...]
    chunk = 512
    for first in range(0, out_s.shape[1], chunk):
        here = slice(first, first + chunk)
        total = lax.dot_general(
            kv_s[:, :half], w_own[here, :], ROWS_ROWS, preferred_element_type=jnp.float32
        ) + lax.dot_general(
            kv_s[:, half:], w_other[here, :], ROWS_ROWS, preferred_element_type=jnp.float32
        )
        out_s[:, here] = total.astype(jnp.bfloat16)
    for step, part in enumerate(parts):
        held = (place[3] - place[5] - step) % count
        part[...] = out_s[pl.ds(pl.multiple_of(held * cap, 64), cap), :]


def input_products(place, own, other, w_own, w_other):
    cap, half = own[0].shape
    count, width = len(own), w_own.shape[0]
    vmem = pl.BlockSpec(memory_space=pltpu.VMEM)

    def body(place, *refs):
        ins, outs, scratch = refs[: 2 * count + 2], refs[2 * count + 2 : 3 * count + 2], refs[3 * count + 2 :]
        products_kernel(place, *ins[: 2 * count], *outs, ins[-2], ins[-1], *scratch)

    return pl.pallas_call(
        body,
        in_specs=[pl.BlockSpec(memory_space=pltpu.SMEM)] + [vmem] * (2 * count + 2),
        out_specs=[vmem] * count,
        out_shape=[jax.ShapeDtypeStruct((cap, width), jnp.bfloat16)] * count,
        scratch_shapes=[
            pltpu.VMEM((count * cap, width), jnp.bfloat16),
            pltpu.VMEM((count * cap, 2 * half), jnp.bfloat16),
        ],
        compiler_params=pltpu.CompilerParams(vmem_limit_bytes=VMEM_BYTES),
        cost_estimate=pl.CostEstimate(
            flops=1_600_000_000, bytes_accessed=6_000_000, transcendentals=0
        ),
        name="input_products",
    )(place, *own, *other, w_own, w_other)


def attention_kernel(counts, place, q_own, do_own, far, kv0, kv1, kv2, kv3,
                     dq_own, dq_far, out0, out1, out2, out3,
                     kv_s, k_s, kt_s, v_s, q_s, do_s, tri_s, s_s, g_s, so_s, go_s, dq_s, dk_s, dv_s, off_s):
    bf, f32 = jnp.bfloat16, jnp.float32
    cap = q_own.shape[0]
    far_heads = far.shape[1] // (2 * HEAD)
    shards = counts.shape[0]
    side = 4
    scale = HEAD**-0.5
    x_at, y_at, group = place[0], place[1], place[2]
    row = lax.broadcasted_iota(jnp.int32, (cap, HEAD), 0)
    lane = lax.broadcasted_iota(jnp.int32, (cap, HEAD), 1)
    zero = jnp.zeros((cap, HEAD), bf)

    def up16(value):
        return ((value + 15) // 16) * 16

    block = side * cap
    for index, ref in enumerate((kv0, kv1, kv2, kv3)):
        kv_s[index * block : (index + 1) * block, :] = ref[...]
    total = jnp.int32(0)
    for s in range(shards):
        off_s[s] = total
        at = pl.ds(pl.multiple_of(total, 16), cap)
        held = ((y_at - s % side) % side) * side + (x_at - s // side) % side
        pair = kv_s[pl.ds(pl.multiple_of(held * cap, 64), cap), :]
        live = row < counts[s]
        k_s[at, :HEAD] = jnp.where(live, pair[:, :HEAD], zero)
        k_s[at, HEAD:] = jnp.where(live, 0.0, jnp.where(lane == 0, MASKED, 0.0)).astype(bf)
        v_s[at, :] = jnp.where(live, pair[:, HEAD:], zero)
        total = total + up16(counts[s])
    end = pl.ds(pl.multiple_of(total, 16), KT)
    k_s[end, :HEAD] = jnp.zeros((KT, HEAD), bf)
    k_s[end, HEAD:] = jnp.zeros((KT, HEAD), bf)
    v_s[end, :] = jnp.zeros((KT, HEAD), bf)

    def k_at(index):
        return pl.ds(pl.multiple_of(index * KT, KT), KT)

    def prepare(j, carry):
        at = k_at(j)
        kt_s[:, at] = k_s[at, :HEAD].T
        dk_s[at, :] = jnp.zeros((KT, HEAD), f32)
        dv_s[at, :] = jnp.zeros((KT, HEAD), f32)
        return carry

    lax.fori_loop(0, (total + cap + KT - 1) // KT, prepare, 0)
    slot = lax.broadcasted_iota(jnp.int32, (cap, 2 * HEAD), 0)
    key_slot = lax.broadcasted_iota(jnp.int32, (cap, 2 * HEAD), 1)
    later = jnp.where(key_slot > slot, MASKED, 0.0).astype(bf)
    same = jnp.where(key_slot == slot, 1.0, 0.0).astype(bf)

    def one_shard(shard, q_ref, do_ref, q_first, do_first, dq_ref):
        count = counts[shard]
        before = pl.multiple_of(off_s[shard], 16)
        rows = up16(count)
        live = row < count
        for h in range(far_heads):
            at = pl.ds(pl.multiple_of(h * rows, 16), cap)
            q_here = pl.ds(pl.multiple_of(q_first + h * HEAD, HEAD), HEAD)
            do_here = pl.ds(pl.multiple_of(do_first + h * HEAD, HEAD), HEAD)
            q_s[at, :] = jnp.where(live, q_ref[:, q_here], zero)
            do_s[at, :] = jnp.where(live, do_ref[:, do_here], zero)
            tri_s[at, :] = later
        tail = pl.ds(pl.multiple_of(far_heads * rows, 16), QT)
        q_s[tail, :] = jnp.zeros((QT, HEAD), bf)
        do_s[tail, :] = jnp.zeros((QT, HEAD), bf)
        tri_s[tail, :] = jnp.zeros((QT, 2 * HEAD), bf)
        own = pl.ds(before, cap)
        full = before // KT
        rest = before - full * KT
        wide = (far_heads * rows + QT - 1) // WIDE
        narrow = (far_heads * rows > wide * WIDE).astype(jnp.int32)

        def query_step(i, carry, size):
            q_at = pl.ds(pl.multiple_of(i * WIDE, WIDE), size)
            one_lane = lax.broadcasted_iota(jnp.int32, (size, HEAD), 1)
            ones = jnp.where(one_lane == 0, 1.0, 0.0).astype(bf)
            key_row = lax.broadcasted_iota(jnp.int32, (KT, size), 0)
            q = q_s[q_at, :]
            do = do_s[q_at, :]
            q_one = jnp.concatenate([q, ones], axis=1)
            own_k = k_s[own, :HEAD]
            scores = lax.dot_general(own_k, q, ROWS_ROWS, preferred_element_type=f32) * (scale * LOG2E)
            scores = scores + lax.dot_general(same, tri_s[q_at, :], ROWS_ROWS, preferred_element_type=f32)
            grads = lax.dot_general(v_s[own, :], do, ROWS_ROWS, preferred_element_type=f32)
            so_s[:, :size] = scores
            go_s[:, :size] = grads
            high = jnp.max(scores, axis=0, keepdims=True)
            e = jnp.exp2(scores - high)
            state = (high, jnp.sum(e, axis=0, keepdims=True), jnp.sum(e * grads, axis=0, keepdims=True))

            def scan(j, state, partial):
                high, total_e, total_w = state
                at = k_at(j)
                scores = lax.dot_general(k_s[at, :], q_one, ROWS_ROWS, preferred_element_type=f32)
                grads = lax.dot_general(v_s[at, :], do, ROWS_ROWS, preferred_element_type=f32)
                scores = scores * (scale * LOG2E)
                if partial:
                    scores = jnp.where(key_row < rest, scores, MASKED)
                s_s[at, :size] = scores
                g_s[at, :size] = grads
                new = jnp.maximum(high, jnp.max(scores, axis=0, keepdims=True))
                e = jnp.exp2(scores - new)
                shrink = jnp.exp2(high - new)
                return (
                    new,
                    total_e * shrink + jnp.sum(e, axis=0, keepdims=True),
                    total_w * shrink + jnp.sum(e * grads, axis=0, keepdims=True),
                )

            state = lax.fori_loop(0, full, functools.partial(scan, partial=False), state)
            ends = full + (rest > 0).astype(jnp.int32)
            high, total_e, total_w = lax.fori_loop(full, ends, functools.partial(scan, partial=True), state)
            delta = total_w / total_e
            log_total = high + jnp.log2(total_e)

            def spread(at, key_t, scores, grads):
                probs = jnp.exp2(scores - log_total)
                dscore = (probs * (grads - delta)).astype(bf)
                dv_s[at, :] += lax.dot_general(probs.astype(bf), do, ROWS_COLS, preferred_element_type=f32)
                dk_s[at, :] += lax.dot_general(dscore, q, ROWS_COLS, preferred_element_type=f32)
                return lax.dot_general(key_t, dscore, ROWS_COLS, preferred_element_type=f32)

            dq = spread(own, own_k.T, so_s[:, :size], go_s[:, :size])
            dq = lax.fori_loop(
                0, ends, lambda j, dq: dq + spread(k_at(j), kt_s[:, k_at(j)], s_s[k_at(j), :size], g_s[k_at(j), :size]), dq
            )
            dq_s[q_at, :] = (dq * scale).T.astype(bf)
            return carry

        lax.fori_loop(0, wide, functools.partial(query_step, size=WIDE), 0)
        lax.fori_loop(wide, wide + narrow, functools.partial(query_step, size=QT), 0)
        for h in range(far_heads):
            at = pl.ds(pl.multiple_of(h * rows, 16), cap)
            dq_ref[:, h * HEAD : (h + 1) * HEAD] = jnp.where(live, dq_s[at, :], zero)

    span = far_heads * HEAD
    one_shard(x_at * side + y_at, q_own, do_own, group * span, group * span, dq_own)
    one_shard((side - 1 - x_at) * side + y_at, far, far, 0, span, dq_far)

    for step, ref in enumerate((out0, out1, out2, out3)):
        for x in range(side):
            shard = x * side + (y_at + step) % side
            at = pl.ds(pl.multiple_of(off_s[shard], 16), cap)
            here = slice(x * cap, (x + 1) * cap)
            live = row < counts[shard]
            ref[here, :HEAD] = jnp.where(live, dk_s[at, :] * scale, 0.0).astype(bf)
            ref[here, HEAD:] = jnp.where(live, dv_s[at, :], 0.0).astype(bf)


def attention_backward(counts, place, q_own, do_own, far, kvs):
    cap, width = far.shape[0], far.shape[1] // 2
    shards = counts.shape[0]
    rows = shards * cap
    keys = -(-(rows + KT) // KT) * KT
    queries = -(-(cap * (width // HEAD) + max(QT, cap)) // QT) * QT
    bf, f32 = jnp.bfloat16, jnp.float32
    vmem = pl.BlockSpec(memory_space=pltpu.VMEM)
    smem = pl.BlockSpec(memory_space=pltpu.SMEM)
    block = kvs[0].shape
    return pl.pallas_call(
        attention_kernel,
        out_shape=[jax.ShapeDtypeStruct((cap, width), bf)] * 2 + [jax.ShapeDtypeStruct(block, bf)] * 4,
        in_specs=[smem, smem] + [vmem] * 7,
        out_specs=[vmem] * 6,
        scratch_shapes=[
            pltpu.VMEM((rows, 2 * HEAD), bf),
            pltpu.VMEM((keys, 2 * HEAD), bf),
            pltpu.VMEM((HEAD, keys), bf),
            pltpu.VMEM((keys, HEAD), bf),
            pltpu.VMEM((queries, HEAD), bf),
            pltpu.VMEM((queries, HEAD), bf),
            pltpu.VMEM((queries, 2 * HEAD), bf),
            pltpu.VMEM((keys, WIDE), f32),
            pltpu.VMEM((keys, WIDE), f32),
            pltpu.VMEM((cap, WIDE), f32),
            pltpu.VMEM((cap, WIDE), f32),
            pltpu.VMEM((queries, HEAD), bf),
            pltpu.VMEM((keys, HEAD), f32),
            pltpu.VMEM((keys, HEAD), f32),
            pltpu.SMEM((shards,), jnp.int32),
        ],
        compiler_params=pltpu.CompilerParams(vmem_limit_bytes=VMEM_BYTES),
        cost_estimate=pl.CostEstimate(flops=6_000_000_000, bytes_accessed=6_000_000, transcendentals=10_000_000),
        name="attention_backward",
    )(counts, place, q_own, do_own, far, *kvs)


def spread_kernel(order, target_ref, *refs):
    parts, (out_ref, pick_ref) = refs[:2], refs[-2:]
    step = pl.program_id(0)
    tokens, capacity = pick_ref.shape

    @pl.when(step == 0)
    def _():
        token = lax.broadcasted_iota(jnp.int32, (tokens, capacity), 0)
        pick_ref[...] = (token == target_ref[...]).astype(jnp.bfloat16)

    for index, part in enumerate(parts):

        @pl.when(step == index)
        def _(part=part):
            out_ref[...] = lax.dot_general(
                pick_ref[...], part[...], ROWS_COLS, preferred_element_type=jnp.float32
            ).astype(jnp.bfloat16)


def spread_rows(order, target, parts, shape, held=()):
    capacity, width = parts[0].shape
    tokens = shape[0]
    whole = pl.BlockSpec((capacity, width), lambda s, order: (0, 0))
    return pl.pallas_call(
        spread_kernel,
        grid_spec=pltpu.PrefetchScalarGridSpec(
            num_scalar_prefetch=1,
            grid=(len(parts),),
            in_specs=[pl.BlockSpec((1, capacity), lambda s, order: (0, 0))]
            + [whole] * len(parts)
            + [pl.BlockSpec(memory_space=pl.ANY)] * len(held),
            out_specs=pl.BlockSpec((tokens, width), lambda s, order: (0, order[s])),
            scratch_shapes=[pltpu.VMEM((tokens, capacity), jnp.bfloat16)],
        ),
        out_shape=jax.ShapeDtypeStruct(shape, jnp.bfloat16),
        input_output_aliases={2 + len(parts): 0} if held else {},
        cost_estimate=pl.CostEstimate(
            flops=400_000_000, bytes_accessed=3_000_000, transcendentals=0
        ),
        name="spread_rows",
    )(order, target[None, :], *parts, *held)


def shards(hidden, kept, counts, queries, keys, values, out_grad, kv_weight):
    f32 = jnp.float32
    seq_devices = lax.axis_size("seq")
    dp_devices = lax.axis_size("dp")
    rep_devices = lax.axis_size("rep")
    seq_index = lax.axis_index("seq")
    dp_index = lax.axis_index("dp")
    rep_index = lax.axis_index("rep")
    capacity = queries.shape[1]
    tokens_local = hidden.shape[1]
    local_groups = keys.shape[2] // HEAD
    group_columns = queries.shape[2] // local_groups
    width = kv_weight.shape[2]
    part_rows = kv_weight.shape[0] // rep_devices
    dp_per_rep = dp_devices // rep_devices
    lane_of = (dp_index % dp_per_rep) * rep_devices + rep_index
    x_at, y_at = seq_index // SIDE, seq_index % SIDE
    group = x_at // (SIDE // local_groups)
    place = jnp.stack([x_at, y_at, group, dp_index, rep_index, lane_of]).astype(jnp.int32)
    swap = [(i, (i + 1) % rep_devices) for i in range(rep_devices)]
    mirror = [(i, (SIDE - 1 - i // SIDE) * SIDE + i % SIDE) for i in range(seq_devices)]

    def shift_dp(array, step):
        return lax.ppermute(array, "dp", [(i, (i + step) % dp_devices) for i in range(dp_devices)])

    def shift_x(array, step):
        pairs = [(i, ((i // SIDE + step) % SIDE) * SIDE + i % SIDE) for i in range(seq_devices)]
        return lax.ppermute(array, "seq", pairs)

    def shift_y(array, step):
        pairs = [(i, (i // SIDE) * SIDE + (i % SIDE + step) % SIDE) for i in range(seq_devices)]
        return lax.ppermute(array, "seq", pairs)

    by_group = [
        jnp.concatenate([keys[0][:, g * HEAD : (g + 1) * HEAD], values[0][:, g * HEAD : (g + 1) * HEAD]], axis=1)
        for g in range(local_groups)
    ]

    def pair_for(step):
        wanted = ((x_at + step) % SIDE) // (SIDE // local_groups)
        chosen = by_group[0]
        for g in range(1, local_groups):
            chosen = jnp.where(wanted == g, by_group[g], chosen)
        return chosen

    kv_x = [pair_for(0)] + [shift_x(pair_for(step), step) for step in range(1, SIDE)]
    kv_x = jnp.concatenate(kv_x, axis=0)
    sent = (1 - group) * group_columns
    far = jnp.concatenate(
        [lax.dynamic_slice_in_dim(array[0], sent, group_columns, 1) for array in (queries, out_grad)], axis=1
    )
    kv_x, far, hidden = lax.optimization_barrier((kv_x, far, hidden))
    kv_y = [kv_x] + [shift_y(kv_x, step) for step in range(1, SIDE)]

    far = lax.ppermute(far, "seq", mirror)

    own_rows = lax.dynamic_index_in_dim(kept[0], seq_index, 0, keepdims=False)
    own_count = lax.dynamic_index_in_dim(counts[0], seq_index, 0, keepdims=False)
    columns = gather_columns(place, own_rows, hidden[0], dp_devices, rep_devices)
    slot_index = jnp.arange(capacity, dtype=jnp.int32)
    target = jnp.where(slot_index < own_count, own_rows, tokens_local)
    kv_y[1:], columns, target = lax.optimization_barrier((kv_y[1:], columns, target))
    columns = lax.all_to_all(columns, "dp", split_axis=0, concat_axis=0, tiled=True)

    grads = attention_backward(counts[0], place, queries[0], out_grad[0], far, kv_y)
    (dq_own, dq_far, *kv_back), columns = lax.optimization_barrier((tuple(grads), columns))
    kv_back = [kv_back[0]] + [shift_y(kv_back[step], step) for step in range(1, SIDE)]
    dq_back = lax.ppermute(dq_far, "seq", mirror)
    columns_far = lax.ppermute(columns, "rep", swap)
    dq_back, kv_weight = lax.optimization_barrier((dq_back, kv_weight))
    halves = kv_weight.reshape(rep_devices, part_rows, 2 * width)
    kept_half = lax.dynamic_index_in_dim(halves, rep_index, 0, keepdims=False)
    sent_half = lax.dynamic_index_in_dim(halves, 1 - rep_index, 0, keepdims=False)
    kv_back[-1], columns_far, kept_half, sent_half = lax.optimization_barrier(
        (kv_back[-1], columns_far, kept_half, sent_half)
    )

    pieces = y_sum(place, kv_back)
    pieces, sent_half = lax.optimization_barrier((pieces, sent_half))
    other_half = lax.ppermute(sent_half, "rep", swap)
    pieces = [pieces[0]] + [shift_x(pieces[step], step) for step in range(1, SIDE)]
    pieces, dq_back, other_half = lax.optimization_barrier((pieces, dq_back, other_half))
    kv_grad = x_sum(place, pieces, local_groups)
    dq_first = jnp.where(group == 0, dq_own, dq_back)
    dq_last = jnp.where(group == 0, dq_back, dq_own)
    back_query = jnp.concatenate([dq_first, dq_last], axis=1)

    kv_all = [kv_grad] + [shift_dp(kv_grad, step) for step in range(1, dp_devices)]
    kv_far = [lax.ppermute(part, "rep", swap) for part in kv_all]
    kv_all, kv_far, back_query = lax.optimization_barrier((kv_all, kv_far, back_query))

    terms = weight_terms(place, columns, columns_far, kv_all)
    terms = lax.all_to_all(
        terms.reshape(seq_devices, -1, 2 * width), "seq", split_axis=0, concat_axis=0, tiled=True
    )
    grad_weight = jnp.sum(terms.astype(f32), axis=0).reshape(-1, 2, width)

    products = input_products(place, kv_all, kv_far, kept_half, other_half)
    received = []
    for step in range(dp_devices):
        pairs = []
        for dp in range(dp_devices):
            for rep in range(rep_devices):
                lane = (dp % dp_per_rep) * rep_devices + rep
                to_dp = (lane + step) % dp_devices
                pairs.append((dp * rep_devices + rep, to_dp * rep_devices + dp // dp_per_rep))
        received.append(lax.ppermute(products[step], ("dp", "rep"), pairs))
    held = ()
    for steps in ((0, 3), (1, 2)):
        order = jnp.stack([(dp_index - step) % dp_devices for step in steps]).astype(jnp.int32)
        parts = [received[step] for step in steps]
        held = (spread_rows(order, target, parts, (tokens_local, dp_devices * part_rows), held),)
    grad_hidden = held[0]
    return (back_query[None], grad_hidden[None], grad_weight)


def solution(mesh):
    placed = (
        P("dp", "seq", None),
        P("dp", None, None),
        P("dp", None),
        P("dp", "seq", "rep"),
        P("dp", "seq", "rep"),
        P("dp", "seq", "rep"),
        P("dp", "seq", "rep"),
        P("dp", None, "rep"),
    )
    return jax.shard_map(
        shards,
        mesh=mesh,
        in_specs=placed,
        out_specs=(P("dp", "seq", "rep"), P("dp", "seq", "rep"), P(("seq", "dp"), None, "rep")),
        check_vma=False,
    )
```

```python
import functools

import jax
import jax.numpy as jnp
from jax import lax
from jax.experimental import pallas as pl
from jax.experimental.pallas import tpu as pltpu
from jax.sharding import PartitionSpec as P

HEAD = 128
MASKED = -1e30
LOG2E = 1.4426950408889634
ROWS_ROWS = (((1,), (1,)), ((), ()))
ROWS_COLS = (((1,), (0,)), ((), ()))
QT = 512
WIDE = 1024
KT = 512
VMEM_BYTES = 56 * 1024 * 1024
SIDE = 4


def gather_kernel(place, rows_ref, hidden_ref, out_ref, pick_ref):
    capacity, tokens = rows_ref.shape[0], hidden_ref.shape[0]

    @pl.when(pl.program_id(0) == 0)
    def _():
        token = lax.broadcasted_iota(jnp.int32, (capacity, tokens), 1)
        pick_ref[...] = (token == rows_ref[...]).astype(jnp.bfloat16)

    picked = lax.dot_general(
        pick_ref[...], hidden_ref[...], ROWS_COLS, preferred_element_type=jnp.float32
    ).astype(jnp.bfloat16)
    parts = out_ref.shape[0]
    for part in range(parts):
        for block in range(out_ref.shape[2] // HEAD):
            first = (block * parts + part) * HEAD
            out_ref[part, :, block * HEAD : (block + 1) * HEAD] = picked[:, first : first + HEAD]


def gather_columns(place, rows, hidden, parts, cores):
    capacity = rows.shape[0]
    tokens, width = hidden.shape
    half = width // cores
    steps = 4
    block = half // steps
    return pl.pallas_call(
        gather_kernel,
        grid_spec=pltpu.PrefetchScalarGridSpec(
            num_scalar_prefetch=1,
            grid=(steps,),
            in_specs=[
                pl.BlockSpec((capacity, 1), lambda s, place: (0, 0)),
                pl.BlockSpec((tokens, block), lambda s, place: (0, place[4] * steps + s)),
            ],
            out_specs=pl.BlockSpec((parts, capacity, block // parts), lambda s, place: (0, 0, s)),
            scratch_shapes=[pltpu.VMEM((capacity, tokens), jnp.bfloat16)],
        ),
        out_shape=jax.ShapeDtypeStruct((parts, capacity, half // parts), hidden.dtype),
        cost_estimate=pl.CostEstimate(
            flops=800_000_000, bytes_accessed=6_000_000, transcendentals=0
        ),
        name="gather_columns",
    )(place, rows[:, None], hidden)


def y_sum_kernel(place, *refs):
    parts, outs = refs[:4], refs[4:]
    cap = outs[0].shape[0]
    for step, out in enumerate(outs):
        at = pl.ds(pl.multiple_of(((place[0] + step) % len(outs)) * cap, 64), cap)
        total = parts[0][at, :].astype(jnp.float32)
        for part in parts[1:]:
            total = total + part[at, :].astype(jnp.float32)
        out[...] = total.astype(jnp.bfloat16)


def y_sum(place, parts):
    rows, width = parts[0].shape
    vmem = pl.BlockSpec(memory_space=pltpu.VMEM)
    return pl.pallas_call(
        y_sum_kernel,
        in_specs=[pl.BlockSpec(memory_space=pltpu.SMEM)] + [vmem] * len(parts),
        out_specs=[vmem] * len(parts),
        out_shape=[jax.ShapeDtypeStruct((rows // len(parts), width), jnp.bfloat16)] * len(parts),
        cost_estimate=pl.CostEstimate(
            flops=1_000_000, bytes_accessed=2_000_000, transcendentals=0
        ),
        name="y_sum",
    )(place, *parts)


def x_sum_kernel(place, *refs):
    parts, out_ref, by_x = refs[:-2], refs[-2], refs[-1]
    cap = out_ref.shape[0]
    count = len(parts)
    groups = out_ref.shape[1] // (2 * HEAD)
    for step, part in enumerate(parts):
        at = pl.ds(pl.multiple_of(((place[0] - step) % count) * cap, 64), cap)
        by_x[at, :] = part[...].astype(jnp.float32)
    size = count // groups
    for group in range(groups):
        total = by_x[group * size * cap : (group * size + 1) * cap, :]
        for x in range(group * size + 1, (group + 1) * size):
            total = total + by_x[x * cap : (x + 1) * cap, :]
        total = total.astype(jnp.bfloat16)
        for kind in range(2):
            first = (kind * groups + group) * HEAD
            out_ref[:, first : first + HEAD] = total[:, kind * HEAD : (kind + 1) * HEAD]


def x_sum(place, parts, groups):
    rows, width = parts[0].shape
    vmem = pl.BlockSpec(memory_space=pltpu.VMEM)
    return pl.pallas_call(
        x_sum_kernel,
        in_specs=[pl.BlockSpec(memory_space=pltpu.SMEM)] + [vmem] * len(parts),
        out_specs=vmem,
        out_shape=jax.ShapeDtypeStruct((rows, groups * width), jnp.bfloat16),
        scratch_shapes=[pltpu.VMEM((rows * len(parts), width), jnp.float32)],
        cost_estimate=pl.CostEstimate(
            flops=1_000_000, bytes_accessed=1_000_000, transcendentals=0
        ),
        name="x_sum",
    )(place, *parts)


def terms_kernel(place, own_ref, other_ref, *refs):
    kv, (out_ref, columns_s, kv_s) = refs[:-3], refs[-3:]
    count, cap = len(kv), kv[0].shape[0]
    step = pl.program_id(0)

    def collect(columns_ref):
        for index in range(count):
            held = (place[3] - index) % count
            columns_s[index * cap : (index + 1) * cap, :] = columns_ref[held]

    @pl.when(step == 0)
    def _():
        collect(own_ref)
        for index, part in enumerate(kv):
            kv_s[index * cap : (index + 1) * cap, :] = part[...]

    @pl.when(step == 1)
    def _():
        collect(other_ref)

    out_ref[...] = lax.dot_general(
        columns_s[...], kv_s[...], (((0,), (0,)), ((), ())), preferred_element_type=jnp.float32
    ).astype(jnp.bfloat16)


def weight_terms(place, own, other, kv):
    count, cap, half = own.shape
    width = kv[0].shape[1]
    columns = pl.BlockSpec((count, cap, half), lambda s, place: (0, 0, 0))
    return pl.pallas_call(
        terms_kernel,
        grid_spec=pltpu.PrefetchScalarGridSpec(
            num_scalar_prefetch=1,
            grid=(2,),
            in_specs=[columns] * 2
            + [pl.BlockSpec((cap, width), lambda s, place: (0, 0))] * len(kv),
            out_specs=pl.BlockSpec((half, width), lambda s, place: ((s + place[4]) % 2, 0)),
            scratch_shapes=[
                pltpu.VMEM((count * cap, half), jnp.bfloat16),
                pltpu.VMEM((count * cap, width), jnp.bfloat16),
            ],
        ),
        out_shape=jax.ShapeDtypeStruct((2 * half, width), jnp.bfloat16),
        compiler_params=pltpu.CompilerParams(vmem_limit_bytes=VMEM_BYTES),
        cost_estimate=pl.CostEstimate(
            flops=1_600_000_000, bytes_accessed=6_000_000, transcendentals=0
        ),
        name="weight_terms",
    )(place, own, other, *kv)


def products_kernel(place, *refs):
    w_own, w_other, out_s, kv_s = refs[-4:]
    count = (len(refs) - 4) // 3
    own, other, parts = refs[:count], refs[count : 2 * count], refs[2 * count : 3 * count]
    cap, half = own[0].shape
    for index in range(count):
        kv_s[index * cap : (index + 1) * cap, :half] = own[index][...]
        kv_s[index * cap : (index + 1) * cap, half:] = other[index][...]
    chunk = 512
    for first in range(0, out_s.shape[1], chunk):
        here = slice(first, first + chunk)
        total = lax.dot_general(
            kv_s[:, :half], w_own[here, :], ROWS_ROWS, preferred_element_type=jnp.float32
        ) + lax.dot_general(
            kv_s[:, half:], w_other[here, :], ROWS_ROWS, preferred_element_type=jnp.float32
        )
        out_s[:, here] = total.astype(jnp.bfloat16)
    for step, part in enumerate(parts):
        held = (place[3] - place[5] - step) % count
        part[...] = out_s[pl.ds(pl.multiple_of(held * cap, 64), cap), :]


def input_products(place, own, other, w_own, w_other):
    cap, half = own[0].shape
    count, width = len(own), w_own.shape[0]
    vmem = pl.BlockSpec(memory_space=pltpu.VMEM)

    def body(place, *refs):
        ins, outs, scratch = refs[: 2 * count + 2], refs[2 * count + 2 : 3 * count + 2], refs[3 * count + 2 :]
        products_kernel(place, *ins[: 2 * count], *outs, ins[-2], ins[-1], *scratch)

    return pl.pallas_call(
        body,
        in_specs=[pl.BlockSpec(memory_space=pltpu.SMEM)] + [vmem] * (2 * count + 2),
        out_specs=[vmem] * count,
        out_shape=[jax.ShapeDtypeStruct((cap, width), jnp.bfloat16)] * count,
        scratch_shapes=[
            pltpu.VMEM((count * cap, width), jnp.bfloat16),
            pltpu.VMEM((count * cap, 2 * half), jnp.bfloat16),
        ],
        compiler_params=pltpu.CompilerParams(vmem_limit_bytes=VMEM_BYTES),
        cost_estimate=pl.CostEstimate(
            flops=1_600_000_000, bytes_accessed=6_000_000, transcendentals=0
        ),
        name="input_products",
    )(place, *own, *other, w_own, w_other)


def attention_kernel(counts, place, q_own, do_own, far, kv0, kv1, kv2, kv3,
                     dq_own, dq_far, out0, out1, out2, out3,
                     kv_s, k_s, kt_s, v_s, q_s, do_s, tri_s, s_s, g_s, so_s, go_s, dq_s, dk_s, dv_s, off_s):
    bf, f32 = jnp.bfloat16, jnp.float32
    cap = q_own.shape[0]
    far_heads = far.shape[1] // (2 * HEAD)
    shards = counts.shape[0]
    side = 4
    scale = HEAD**-0.5
    x_at, y_at, group = place[0], place[1], place[2]
    row = lax.broadcasted_iota(jnp.int32, (cap, HEAD), 0)
    lane = lax.broadcasted_iota(jnp.int32, (cap, HEAD), 1)
    zero = jnp.zeros((cap, HEAD), bf)

    def up16(value):
        return ((value + 15) // 16) * 16

    block = side * cap
    for index, ref in enumerate((kv0, kv1, kv2, kv3)):
        kv_s[index * block : (index + 1) * block, :] = ref[...]
    total = jnp.int32(0)
    for s in range(shards):
        off_s[s] = total
        at = pl.ds(pl.multiple_of(total, 16), cap)
        held = ((y_at - s % side) % side) * side + (x_at - s // side) % side
        pair = kv_s[pl.ds(pl.multiple_of(held * cap, 64), cap), :]
        live = row < counts[s]
        k_s[at, :HEAD] = jnp.where(live, pair[:, :HEAD], zero)
        k_s[at, HEAD:] = jnp.where(live, 0.0, jnp.where(lane == 0, MASKED, 0.0)).astype(bf)
        v_s[at, :] = jnp.where(live, pair[:, HEAD:], zero)
        total = total + up16(counts[s])
    end = pl.ds(pl.multiple_of(total, 16), KT)
    k_s[end, :HEAD] = jnp.zeros((KT, HEAD), bf)
    k_s[end, HEAD:] = jnp.zeros((KT, HEAD), bf)
    v_s[end, :] = jnp.zeros((KT, HEAD), bf)

    def k_at(index):
        return pl.ds(pl.multiple_of(index * KT, KT), KT)

    def prepare(j, carry):
        at = k_at(j)
        kt_s[:, at] = k_s[at, :HEAD].T
        dk_s[at, :] = jnp.zeros((KT, HEAD), f32)
        dv_s[at, :] = jnp.zeros((KT, HEAD), f32)
        return carry

    lax.fori_loop(0, (total + cap + KT - 1) // KT, prepare, 0)
    slot = lax.broadcasted_iota(jnp.int32, (cap, 2 * HEAD), 0)
    key_slot = lax.broadcasted_iota(jnp.int32, (cap, 2 * HEAD), 1)
    later = jnp.where(key_slot > slot, MASKED, 0.0).astype(bf)
    same = jnp.where(key_slot == slot, 1.0, 0.0).astype(bf)

    def one_shard(shard, q_ref, do_ref, q_first, do_first, dq_ref):
        count = counts[shard]
        before = pl.multiple_of(off_s[shard], 16)
        rows = up16(count)
        live = row < count
        for h in range(far_heads):
            at = pl.ds(pl.multiple_of(h * rows, 16), cap)
            q_here = pl.ds(pl.multiple_of(q_first + h * HEAD, HEAD), HEAD)
            do_here = pl.ds(pl.multiple_of(do_first + h * HEAD, HEAD), HEAD)
            q_s[at, :] = jnp.where(live, q_ref[:, q_here], zero)
            do_s[at, :] = jnp.where(live, do_ref[:, do_here], zero)
            tri_s[at, :] = later
        tail = pl.ds(pl.multiple_of(far_heads * rows, 16), QT)
        q_s[tail, :] = jnp.zeros((QT, HEAD), bf)
        do_s[tail, :] = jnp.zeros((QT, HEAD), bf)
        tri_s[tail, :] = jnp.zeros((QT, 2 * HEAD), bf)
        own = pl.ds(before, cap)
        full = before // KT
        rest = before - full * KT
        wide = (far_heads * rows + QT - 1) // WIDE
        narrow = (far_heads * rows > wide * WIDE).astype(jnp.int32)

        def query_step(i, carry, size):
            q_at = pl.ds(pl.multiple_of(i * WIDE, WIDE), size)
            one_lane = lax.broadcasted_iota(jnp.int32, (size, HEAD), 1)
            ones = jnp.where(one_lane == 0, 1.0, 0.0).astype(bf)
            key_row = lax.broadcasted_iota(jnp.int32, (KT, size), 0)
            q = q_s[q_at, :]
            do = do_s[q_at, :]
            q_one = jnp.concatenate([q, ones], axis=1)
            own_k = k_s[own, :HEAD]
            scores = lax.dot_general(own_k, q, ROWS_ROWS, preferred_element_type=f32) * (scale * LOG2E)
            scores = scores + lax.dot_general(same, tri_s[q_at, :], ROWS_ROWS, preferred_element_type=f32)
            grads = lax.dot_general(v_s[own, :], do, ROWS_ROWS, preferred_element_type=f32)
            so_s[:, :size] = scores
            go_s[:, :size] = grads
            high = jnp.max(scores, axis=0, keepdims=True)
            e = jnp.exp2(scores - high)
            state = (high, jnp.sum(e, axis=0, keepdims=True), jnp.sum(e * grads, axis=0, keepdims=True))

            def scan(j, state, tile, partial):
                high, total_e, total_w = state
                at = pl.ds(pl.multiple_of(j * KT, KT), tile)
                scores = lax.dot_general(k_s[at, :], q_one, ROWS_ROWS, preferred_element_type=f32)
                grads = lax.dot_general(v_s[at, :], do, ROWS_ROWS, preferred_element_type=f32)
                scores = scores * (scale * LOG2E)
                if partial:
                    scores = jnp.where(key_row[:tile] < rest, scores, MASKED)
                s_s[at, :size] = scores
                g_s[at, :size] = grads
                new = jnp.maximum(high, jnp.max(scores, axis=0, keepdims=True))
                e = jnp.exp2(scores - new)
                shrink = jnp.exp2(high - new)
                return (
                    new,
                    total_e * shrink + jnp.sum(e, axis=0, keepdims=True),
                    total_w * shrink + jnp.sum(e * grads, axis=0, keepdims=True),
                )

            state = lax.fori_loop(0, full, functools.partial(scan, tile=KT, partial=False), state)
            ends = full + (rest > KT // 2).astype(jnp.int32)
            small = ((rest > 0) & (rest <= KT // 2)).astype(jnp.int32)
            state = lax.fori_loop(full, ends, functools.partial(scan, tile=KT, partial=True), state)
            high, total_e, total_w = lax.fori_loop(
                full, full + small, functools.partial(scan, tile=KT // 2, partial=True), state
            )
            delta = total_w / total_e
            log_total = high + jnp.log2(total_e)

            def spread(at, key_t, scores, grads):
                probs = jnp.exp2(scores - log_total)
                dscore = (probs * (grads - delta)).astype(bf)
                dv_s[at, :] += lax.dot_general(probs.astype(bf), do, ROWS_COLS, preferred_element_type=f32)
                dk_s[at, :] += lax.dot_general(dscore, q, ROWS_COLS, preferred_element_type=f32)
                return lax.dot_general(key_t, dscore, ROWS_COLS, preferred_element_type=f32)

            dq = spread(own, own_k.T, so_s[:, :size], go_s[:, :size])
            def spread_tile(j, dq, tile):
                at = pl.ds(pl.multiple_of(j * KT, KT), tile)
                return dq + spread(at, kt_s[:, at], s_s[at, :size], g_s[at, :size])

            dq = lax.fori_loop(0, ends, functools.partial(spread_tile, tile=KT), dq)
            dq = lax.fori_loop(full, full + small, functools.partial(spread_tile, tile=KT // 2), dq)
            dq_s[q_at, :] = (dq * scale).T.astype(bf)
            return carry

        lax.fori_loop(0, wide, functools.partial(query_step, size=WIDE), 0)
        lax.fori_loop(wide, wide + narrow, functools.partial(query_step, size=QT), 0)
        for h in range(far_heads):
            at = pl.ds(pl.multiple_of(h * rows, 16), cap)
            dq_ref[:, h * HEAD : (h + 1) * HEAD] = jnp.where(live, dq_s[at, :], zero)

    span = far_heads * HEAD
    one_shard(x_at * side + y_at, q_own, do_own, group * span, group * span, dq_own)
    one_shard((side - 1 - x_at) * side + y_at, far, far, 0, span, dq_far)

    for step, ref in enumerate((out0, out1, out2, out3)):
        for x in range(side):
            shard = x * side + (y_at + step) % side
            at = pl.ds(pl.multiple_of(off_s[shard], 16), cap)
            here = slice(x * cap, (x + 1) * cap)
            live = row < counts[shard]
            ref[here, :HEAD] = jnp.where(live, dk_s[at, :] * scale, 0.0).astype(bf)
            ref[here, HEAD:] = jnp.where(live, dv_s[at, :], 0.0).astype(bf)


def attention_backward(counts, place, q_own, do_own, far, kvs):
    cap, width = far.shape[0], far.shape[1] // 2
    shards = counts.shape[0]
    rows = shards * cap
    keys = -(-(rows + KT) // KT) * KT
    queries = -(-(cap * (width // HEAD) + max(QT, cap)) // QT) * QT
    bf, f32 = jnp.bfloat16, jnp.float32
    vmem = pl.BlockSpec(memory_space=pltpu.VMEM)
    smem = pl.BlockSpec(memory_space=pltpu.SMEM)
    block = kvs[0].shape
    return pl.pallas_call(
        attention_kernel,
        out_shape=[jax.ShapeDtypeStruct((cap, width), bf)] * 2 + [jax.ShapeDtypeStruct(block, bf)] * 4,
        in_specs=[smem, smem] + [vmem] * 7,
        out_specs=[vmem] * 6,
        scratch_shapes=[
            pltpu.VMEM((rows, 2 * HEAD), bf),
            pltpu.VMEM((keys, 2 * HEAD), bf),
            pltpu.VMEM((HEAD, keys), bf),
            pltpu.VMEM((keys, HEAD), bf),
            pltpu.VMEM((queries, HEAD), bf),
            pltpu.VMEM((queries, HEAD), bf),
            pltpu.VMEM((queries, 2 * HEAD), bf),
            pltpu.VMEM((keys, WIDE), f32),
            pltpu.VMEM((keys, WIDE), f32),
            pltpu.VMEM((cap, WIDE), f32),
            pltpu.VMEM((cap, WIDE), f32),
            pltpu.VMEM((queries, HEAD), bf),
            pltpu.VMEM((keys, HEAD), f32),
            pltpu.VMEM((keys, HEAD), f32),
            pltpu.SMEM((shards,), jnp.int32),
        ],
        compiler_params=pltpu.CompilerParams(vmem_limit_bytes=VMEM_BYTES),
        cost_estimate=pl.CostEstimate(flops=6_000_000_000, bytes_accessed=6_000_000, transcendentals=10_000_000),
        name="attention_backward",
    )(counts, place, q_own, do_own, far, *kvs)


def spread_kernel(order, target_ref, *refs):
    parts, (out_ref, pick_ref) = refs[:2], refs[-2:]
    step = pl.program_id(0)
    tokens, capacity = pick_ref.shape

    @pl.when(step == 0)
    def _():
        token = lax.broadcasted_iota(jnp.int32, (tokens, capacity), 0)
        pick_ref[...] = (token == target_ref[...]).astype(jnp.bfloat16)

    for index, part in enumerate(parts):

        @pl.when(step == index)
        def _(part=part):
            out_ref[...] = lax.dot_general(
                pick_ref[...], part[...], ROWS_COLS, preferred_element_type=jnp.float32
            ).astype(jnp.bfloat16)


def spread_rows(order, target, parts, shape, held=()):
    capacity, width = parts[0].shape
    tokens = shape[0]
    whole = pl.BlockSpec((capacity, width), lambda s, order: (0, 0))
    return pl.pallas_call(
        spread_kernel,
        grid_spec=pltpu.PrefetchScalarGridSpec(
            num_scalar_prefetch=1,
            grid=(len(parts),),
            in_specs=[pl.BlockSpec((1, capacity), lambda s, order: (0, 0))]
            + [whole] * len(parts)
            + [pl.BlockSpec(memory_space=pl.ANY)] * len(held),
            out_specs=pl.BlockSpec((tokens, width), lambda s, order: (0, order[s])),
            scratch_shapes=[pltpu.VMEM((tokens, capacity), jnp.bfloat16)],
        ),
        out_shape=jax.ShapeDtypeStruct(shape, jnp.bfloat16),
        input_output_aliases={2 + len(parts): 0} if held else {},
        cost_estimate=pl.CostEstimate(
            flops=400_000_000, bytes_accessed=3_000_000, transcendentals=0
        ),
        name="spread_rows",
    )(order, target[None, :], *parts, *held)


def shards(hidden, kept, counts, queries, keys, values, out_grad, kv_weight):
    f32 = jnp.float32
    seq_devices = lax.axis_size("seq")
    dp_devices = lax.axis_size("dp")
    rep_devices = lax.axis_size("rep")
    seq_index = lax.axis_index("seq")
    dp_index = lax.axis_index("dp")
    rep_index = lax.axis_index("rep")
    capacity = queries.shape[1]
    tokens_local = hidden.shape[1]
    local_groups = keys.shape[2] // HEAD
    group_columns = queries.shape[2] // local_groups
    width = kv_weight.shape[2]
    part_rows = kv_weight.shape[0] // rep_devices
    dp_per_rep = dp_devices // rep_devices
    lane_of = (dp_index % dp_per_rep) * rep_devices + rep_index
    x_at, y_at = seq_index // SIDE, seq_index % SIDE
    group = x_at // (SIDE // local_groups)
    place = jnp.stack([x_at, y_at, group, dp_index, rep_index, lane_of]).astype(jnp.int32)
    swap = [(i, (i + 1) % rep_devices) for i in range(rep_devices)]
    mirror = [(i, (SIDE - 1 - i // SIDE) * SIDE + i % SIDE) for i in range(seq_devices)]

    def shift_dp(array, step):
        return lax.ppermute(array, "dp", [(i, (i + step) % dp_devices) for i in range(dp_devices)])

    def shift_x(array, step):
        pairs = [(i, ((i // SIDE + step) % SIDE) * SIDE + i % SIDE) for i in range(seq_devices)]
        return lax.ppermute(array, "seq", pairs)

    def shift_y(array, step):
        pairs = [(i, (i // SIDE) * SIDE + (i % SIDE + step) % SIDE) for i in range(seq_devices)]
        return lax.ppermute(array, "seq", pairs)

    by_group = [
        jnp.concatenate([keys[0][:, g * HEAD : (g + 1) * HEAD], values[0][:, g * HEAD : (g + 1) * HEAD]], axis=1)
        for g in range(local_groups)
    ]

    def pair_for(step):
        wanted = ((x_at + step) % SIDE) // (SIDE // local_groups)
        chosen = by_group[0]
        for g in range(1, local_groups):
            chosen = jnp.where(wanted == g, by_group[g], chosen)
        return chosen

    kv_x = [pair_for(0)] + [shift_x(pair_for(step), step) for step in range(1, SIDE)]
    kv_x = jnp.concatenate(kv_x, axis=0)
    sent = (1 - group) * group_columns
    far = jnp.concatenate(
        [lax.dynamic_slice_in_dim(array[0], sent, group_columns, 1) for array in (queries, out_grad)], axis=1
    )
    kv_x, far, hidden = lax.optimization_barrier((kv_x, far, hidden))
    kv_y = [kv_x] + [shift_y(kv_x, step) for step in range(1, SIDE)]

    far = lax.ppermute(far, "seq", mirror)

    own_rows = lax.dynamic_index_in_dim(kept[0], seq_index, 0, keepdims=False)
    own_count = lax.dynamic_index_in_dim(counts[0], seq_index, 0, keepdims=False)
    columns = gather_columns(place, own_rows, hidden[0], dp_devices, rep_devices)
    slot_index = jnp.arange(capacity, dtype=jnp.int32)
    target = jnp.where(slot_index < own_count, own_rows, tokens_local)
    kv_y[1:], columns, target = lax.optimization_barrier((kv_y[1:], columns, target))
    columns = lax.all_to_all(columns, "dp", split_axis=0, concat_axis=0, tiled=True)

    grads = attention_backward(counts[0], place, queries[0], out_grad[0], far, kv_y)
    (dq_own, dq_far, *kv_back), columns = lax.optimization_barrier((tuple(grads), columns))
    kv_back = [kv_back[0]] + [shift_y(kv_back[step], step) for step in range(1, SIDE)]
    dq_back = lax.ppermute(dq_far, "seq", mirror)
    columns_far = lax.ppermute(columns, "rep", swap)
    dq_back, kv_weight = lax.optimization_barrier((dq_back, kv_weight))
    halves = kv_weight.reshape(rep_devices, part_rows, 2 * width)
    kept_half = lax.dynamic_index_in_dim(halves, rep_index, 0, keepdims=False)
    sent_half = lax.dynamic_index_in_dim(halves, 1 - rep_index, 0, keepdims=False)
    kv_back[-1], columns_far, kept_half, sent_half = lax.optimization_barrier(
        (kv_back[-1], columns_far, kept_half, sent_half)
    )

    pieces = y_sum(place, kv_back)
    pieces, sent_half = lax.optimization_barrier((pieces, sent_half))
    other_half = lax.ppermute(sent_half, "rep", swap)
    pieces = [pieces[0]] + [shift_x(pieces[step], step) for step in range(1, SIDE)]
    pieces, dq_back, other_half = lax.optimization_barrier((pieces, dq_back, other_half))
    kv_grad = x_sum(place, pieces, local_groups)
    dq_first = jnp.where(group == 0, dq_own, dq_back)
    dq_last = jnp.where(group == 0, dq_back, dq_own)
    back_query = jnp.concatenate([dq_first, dq_last], axis=1)

    kv_all = [kv_grad] + [shift_dp(kv_grad, step) for step in range(1, dp_devices)]
    kv_far = [lax.ppermute(part, "rep", swap) for part in kv_all]
    kv_all, kv_far, back_query = lax.optimization_barrier((kv_all, kv_far, back_query))

    terms = weight_terms(place, columns, columns_far, kv_all)
    terms = lax.all_to_all(
        terms.reshape(seq_devices, -1, 2 * width), "seq", split_axis=0, concat_axis=0, tiled=True
    )
    grad_weight = jnp.sum(terms.astype(f32), axis=0).reshape(-1, 2, width)

    products = input_products(place, kv_all, kv_far, kept_half, other_half)
    received = []
    for step in range(dp_devices):
        pairs = []
        for dp in range(dp_devices):
            for rep in range(rep_devices):
                lane = (dp % dp_per_rep) * rep_devices + rep
                to_dp = (lane + step) % dp_devices
                pairs.append((dp * rep_devices + rep, to_dp * rep_devices + dp // dp_per_rep))
        received.append(lax.ppermute(products[step], ("dp", "rep"), pairs))
    held = ()
    for steps in ((0, 3), (1, 2)):
        order = jnp.stack([(dp_index - step) % dp_devices for step in steps]).astype(jnp.int32)
        parts = [received[step] for step in steps]
        held = (spread_rows(order, target, parts, (tokens_local, dp_devices * part_rows), held),)
    grad_hidden = held[0]
    return (back_query[None], grad_hidden[None], grad_weight)


def solution(mesh):
    placed = (
        P("dp", "seq", None),
        P("dp", None, None),
        P("dp", None),
        P("dp", "seq", "rep"),
        P("dp", "seq", "rep"),
        P("dp", "seq", "rep"),
        P("dp", "seq", "rep"),
        P("dp", None, "rep"),
    )
    return jax.shard_map(
        shards,
        mesh=mesh,
        in_specs=placed,
        out_specs=(P("dp", "seq", "rep"), P("dp", "seq", "rep"), P(("seq", "dp"), None, "rep")),
        check_vma=False,
    )
```
